512 devices in a mesh: lat: 64 (over z, x, y_hi), lon: 8 (over y_lo, core).
Axes of the slice: x: 4, y: 8 (y_hi: 2, y_lo: 4; y = y_hi * 4 + y_lo), z: 8, core: 2. Of those that a mesh axis runs over, the one named last changes fastest.
Arguments:
- elevation: float32 [1, 3072, 8640], P(None, 'lat', 'lon'), may hold values from -30 to 30
- velocity: float32 [1, 2, 3072, 8640], P(None, None, 'lat', 'lon'), may hold values from -3 to 3
- wind_forcing: float32 [2, 3072, 8640], P(None, 'lat', 'lon'), may hold values from -0.6 to 0.6
- ocean_depth: float32 [3072, 8640], P('lat', 'lon'), may hold values from 0.2 to 1
- wet_mask: int32 [3072, 8640], P('lat', 'lon'), may hold values from 0 to 1, as said below
- love_factor: float32 [1081], replicated, may hold values from 0.3 to 3
- wavenumbers: int32 [64], replicated, may hold values from 0 to 127, as said below
Outputs:
- new_elevation: float32 [1, 3072, 8640], P(None, 'lat', 'lon')
- new_velocity: float32 [1, 2, 3072, 8640], P(None, None, 'lat', 'lon')
- self_loading: float32 [1, 3072, 8640], P(None, 'lat', 'lon')
The draws below stay inside these ranges and needn't reach their ends.
Inputs may be any that keep to these rules, and one draw needn't show every extreme that they name: `wet_mask`: 0 in the 24 rows nearest each pole. `wavenumbers`: distinct.
All inputs are finite; a program needn't handle non-finite values.
Results may differ from the reference program's by a relative error of at most 0.0003.
Values sent between devices are 32-bit elements; how exact they have to be, the bound alone decides.
A program may use at most 64 MiB of HBM per device.

```python
import math
import jax
import jax.numpy as jnp
from jax import lax

GRID_LAT = 3072
GRID_LON = 8640
DEGREES = 1081
MEMBERS = 1
TIME_STEPS = 1
WAVE_SET = 64


def window_numbers(key):
    pool_size = min(DEGREES, 2 * WAVE_SET)
    return jax.random.permutation(jax.random.fold_in(key, 7), pool_size)[:WAVE_SET].astype(jnp.int32)


def draw_elevation(key, part):
    keys = jax.random.split(key, 6)
    wave_orders = jax.random.randint(keys[0], (16,), 0, 16)
    lat_orders = jax.random.randint(keys[1], (16,), 0, 7)
    amplitude = jax.random.uniform(keys[2], (MEMBERS, 16), jnp.float32, -1.2, 1.2)
    phases = jax.random.uniform(keys[3], (MEMBERS, 16), jnp.float32, 0.0, 2.0 * jnp.pi)
    polar_angle = jnp.pi * (jnp.arange(GRID_LAT).astype(jnp.float32) + 0.5) / GRID_LAT
    longitude = 2.0 * jnp.pi * jnp.arange(GRID_LON).astype(jnp.float32) / GRID_LON
    profile = jnp.cos(lat_orders.astype(jnp.float32)[:, None] * polar_angle[None, :])
    cosines = jnp.cos(wave_orders.astype(jnp.float32)[:, None] * longitude[None, :])
    sines = jnp.sin(wave_orders.astype(jnp.float32)[:, None] * longitude[None, :])
    left_cos = (amplitude * jnp.cos(phases))[:, :, None] * profile[None]
    left_sin = (amplitude * jnp.sin(phases))[:, :, None] * profile[None]
    smooth = jnp.einsum('ecj,ck->ejk', left_cos, cosines) - jnp.einsum('ecj,ck->ejk', left_sin, sines)
    window = window_numbers(key)
    window_phase = window[:, None] * jnp.arange(GRID_LON, dtype=jnp.int32)[None, :] % GRID_LON
    window_angle = 2.0 * jnp.pi / GRID_LON * window_phase.astype(jnp.float32)
    window_cos = jnp.cos(window_angle)
    window_sin = jnp.sin(window_angle)
    shape = (MEMBERS, GRID_LAT, GRID_LON)
    profile_shape = (MEMBERS, 2, WAVE_SET, GRID_LAT)
    rows_rough = jax.random.truncated_normal(keys[5], -3.0, 3.0, profile_shape, jnp.float32)
    banded = jnp.einsum('ewj,wk->ejk', rows_rough[:, 0], window_cos) + jnp.einsum('ewj,wk->ejk', rows_rough[:, 1], window_sin)
    rough = 0.3 * jax.random.truncated_normal(keys[4], -3.0, 3.0, shape, jnp.float32)
    total = smooth + rough + banded
    return jnp.clip(total, -30.0, 30.0)


def draw_wet_mask(key, part):
    rows_index = jnp.arange(GRID_LAT, dtype=jnp.int32)[:, None]
    polar_cap = GRID_LAT // 128
    coins = jax.random.randint(key, (GRID_LAT, GRID_LON), 0, 5)
    wet = (coins < 4) & (rows_index >= polar_cap) & (rows_index < GRID_LAT - polar_cap)
    return wet.astype(jnp.int32)


def draw_wavenumbers(key, part):
    return window_numbers(key)


def level_of(key, shape, cuts, smallest, high):
    def one(dim, parts):
        draws = jax.random.uniform(jax.random.fold_in(jax.random.fold_in(key, 6), dim), (parts,), jnp.float32, smallest / len(cuts), high / len(cuts))
        return jnp.repeat(jnp.exp(draws), shape[dim] // parts).reshape((-1,) + (1,) * (len(shape) - dim - 1))

    level = one(*cuts[0])
    for cut in cuts[1:]:
        level = level * one(*cut)
    return level


def centred(stream_key, dims, width, limit, cuts=(), kind=jnp.bfloat16):
    drawn = width * jax.random.normal(stream_key, dims, jnp.float32)
    if cuts:
        drawn = drawn * level_of(stream_key, dims, cuts, -0.22, 0.18)
    return jnp.clip(drawn, -limit, limit).astype(kind)


def setup_inputs(seed: int = 0) -> dict:
    key_list = jax.random.split(jax.random.key(seed), 8)
    return {
        "elevation": draw_elevation(jax.random.fold_in(key_list[7], 71), 0),
        "velocity": centred(key_list[1], (MEMBERS, 2, GRID_LAT, GRID_LON), 0.5, 3.0, ((2, 64), (3, 8)), jnp.float32),
        "wind_forcing": centred(key_list[2], (2, GRID_LAT, GRID_LON), 0.1, 0.6, ((1, 64), (2, 8)), jnp.float32),
        "ocean_depth": jnp.clip(jnp.exp(math.log(1.0) - 1.609438 * jax.random.uniform(key_list[3], (GRID_LAT, GRID_LON), jnp.float32) ** level_of(key_list[3], (GRID_LAT, GRID_LON), ((0, 64), (1, 8)), -0.2, 0.2)), 0.2, 1.0),
        "wet_mask": draw_wet_mask(jax.random.fold_in(key_list[7], 71), 0),
        "love_factor": jnp.clip(jnp.exp(jax.random.uniform(key_list[5], (DEGREES,), jnp.float32, math.log(0.3), math.log(3.0))), 0.3, 3.0),
        "wavenumbers": draw_wavenumbers(jax.random.fold_in(key_list[7], 71), 0),
    }


friction_rate = 0.1
step_ratio = 0.05
highest = lax.Precision.HIGHEST

def colatitude(rows_index):
    return jnp.pi * (rows_index.astype(jnp.float32) + 0.5) / GRID_LAT

def legendre(orders, cosine, sine_row, length):
    real_type = cosine.dtype
    order_real = orders.astype(real_type)
    ladder = jnp.arange(2, length + 1).astype(real_type)
    summands = jnp.where(ladder[None, :] <= order_real, jnp.log((2.0 * ladder + 1.0) / (2.0 * ladder))[None, :], 0.0)
    log_start = 0.5 * (jnp.where(order_real > 0.0, jnp.log(3.0), 0.0) + lax.optimization_barrier(jnp.sum(summands, axis=1, keepdims=True))) + order_real * jnp.log(sine_row)
    current = jnp.ones(log_start.shape, real_type)
    previous = jnp.zeros(log_start.shape, real_type)

    def recur(carried, degree):
        current, previous, log_scale = carried
        degree_real = degree.astype(real_type)
        active = degree_real > order_real
        raising = jnp.sqrt(jnp.maximum(4.0 * degree_real * degree_real - 1.0, 0.0) / jnp.maximum(degree_real * degree_real - order_real * order_real, 1.0))
        lower_degree = degree_real - 1.0
        lowering = jnp.sqrt(jnp.maximum(lower_degree * lower_degree - order_real * order_real, 0.0) / jnp.maximum(4.0 * lower_degree * lower_degree - 1.0, 1.0))
        latest = raising * (cosine * current - lowering * previous)
        current_next = jnp.where(active, latest, current)
        previous_next = jnp.where(active, current, previous)
        result = jnp.where(degree_real >= order_real, current_next * jnp.exp(log_scale), 0.0)
        magnitude = jnp.abs(current_next) + jnp.abs(previous_next)
        return ((current_next / magnitude, previous_next / magnitude, log_scale + jnp.log(magnitude)), result)
    _, values = lax.scan(recur, (current, previous, log_start), jnp.arange(length, dtype=jnp.int32), unroll=8)
    return values

def fourier_tables(waves, columns):
    phase = waves[None, :] * columns[:, None] % GRID_LON
    angle = 2.0 * jnp.pi / GRID_LON * phase.astype(jnp.float32)
    cosines = jnp.cos(angle)
    sines = jnp.sin(angle)
    forward = jnp.stack([cosines, sines], axis=-1).reshape(columns.shape[0], 2 * waves.shape[0]) / GRID_LON
    inverse = jnp.stack([cosines.T, sines.T], axis=1).reshape(2 * waves.shape[0], columns.shape[0])
    return (forward, inverse)

def loading_field(elevation, wet_float, love_factor, wavenumbers):
    members = elevation.shape[0]
    wave_total = wavenumbers.shape[0]
    forward, inverse = fourier_tables(wavenumbers, jnp.arange(GRID_LON, dtype=jnp.int32))
    load_mass = wet_float[None] * elevation
    fourier = jnp.dot(load_mass.reshape(members * GRID_LAT, GRID_LON), forward, precision=highest).reshape(members, GRID_LAT, 2 * wave_total)
    polar_angle = colatitude(jnp.arange(GRID_LAT, dtype=jnp.int32))
    cosine = jnp.cos(polar_angle)
    sine_row = jnp.sin(polar_angle)
    weights = jnp.pi * sine_row / (2.0 * GRID_LAT)
    love_weight = love_factor / (2.0 * jnp.arange(DEGREES).astype(jnp.float32) + 1.0)

    def one_wave(position):
        orders = lax.dynamic_slice_in_dim(wavenumbers, position, 1).reshape(1, 1)
        tables = legendre(orders, cosine[None, :], sine_row[None, :], DEGREES)[:, 0, :]
        wave_slab = lax.dynamic_slice_in_dim(fourier, 2 * position, 2, axis=2) * weights[None, :, None]
        coeffs = jnp.einsum('lr,erc->ecl', tables, wave_slab, precision=highest)
        return jnp.einsum('lr,ecl->erc', tables, coeffs * love_weight, precision=highest)
    spectral = lax.map(one_wave, jnp.arange(wave_total, dtype=jnp.int32))
    spectral = jnp.transpose(spectral, (1, 2, 0, 3)).reshape(members * GRID_LAT, 2 * wave_total)
    return jnp.dot(spectral, inverse, precision=highest).reshape(members, GRID_LAT, GRID_LON)

def advance(elevation, velocity, wind_push, inverse_depth, ocean_depth, wet_float, loading):
    surface = elevation - loading
    sine_row = jnp.sin(colatitude(jnp.arange(GRID_LAT, dtype=jnp.int32)))
    zonal_step = (step_ratio / sine_row)[:, None]
    meridional = 0.1 * GRID_LAT / GRID_LON
    eastward = velocity[:, 0]
    southward = velocity[:, 1]
    zonal_change = jnp.roll(surface, -1, axis=2) - jnp.roll(surface, 1, axis=2)
    padded = jnp.pad(surface, ((0, 0), (1, 1), (0, 0)))
    merid_change = padded[:, 2:] - padded[:, :-2]
    damping = 1.0 + friction_rate * jnp.sqrt(eastward * eastward + southward * southward) * inverse_depth
    east_next = wet_float * (eastward + wind_push[0] - zonal_step * zonal_change) / damping
    south_next = wet_float * (southward + wind_push[1] - meridional * merid_change) / damping
    east_flux = ocean_depth * east_next
    south_flux = sine_row[:, None] * ocean_depth * south_next
    padded_flux = jnp.pad(south_flux, ((0, 0), (1, 1), (0, 0)))
    tendency = zonal_step * (jnp.roll(east_flux, -1, axis=2) - jnp.roll(east_flux, 1, axis=2)) + (meridional / sine_row)[:, None] * (padded_flux[:, 2:] - padded_flux[:, :-2])
    elevation_next = elevation - wet_float * tendency
    return (elevation_next, jnp.stack([east_next, south_next], axis=1))

def reference(elevation, velocity, wind_forcing, ocean_depth, wet_mask, love_factor, wavenumbers):
    wet_float = wet_mask.astype(jnp.float32)
    wind_push = wind_forcing / ocean_depth[None]
    inverse_depth = 1.0 / ocean_depth
    elevation_now = elevation
    velocity_now = velocity
    loading = jnp.zeros_like(elevation)
    for _ in range(TIME_STEPS):
        loading = loading_field(elevation_now, wet_float, love_factor, wavenumbers)
        elevation_now, velocity_now = advance(elevation_now, velocity_now, wind_push, inverse_depth, ocean_depth, wet_float, loading)
    return (elevation_now, velocity_now, loading)
```

```python
import functools
import math

import jax
import jax.numpy as jnp
from jax import lax
from jax.experimental import pallas as pl
from jax.experimental.pallas import tpu as pltpu
from jax.sharding import PartitionSpec as P

GRID_LAT = 3072
GRID_LON = 8640
DEGREES = 1081
STEP_RATIO = 0.05
FRICTION = 0.1

BAND = 48
SLOT = 64
PAIR = 8
F32 = jnp.float32
BF16 = jnp.bfloat16
MESH = pl.DeviceIdType.MESH


def iota(shape, dim):
    return lax.broadcasted_iota(jnp.int32, shape, dim)


def halves(x):
    high = x.astype(BF16)
    return high, (x - high.astype(F32)).astype(BF16)


def rows_dot(a, b):
    return lax.dot_general(a, b, (((1,), (0,)), ((), ())), preferred_element_type=F32)


def rows_dot_t(a, b):
    return lax.dot_general(a, b, (((1,), (1,)), ((), ())), preferred_element_type=F32)


def circle(phase, period):
    turns = jnp.floor(phase * (4.0 / period) + 0.5)
    t = (phase - turns * (period / 4.0)) * (2.0 * math.pi / period)
    t2 = t * t
    s = t * (1.0 + t2 * (-1.0 / 6 + t2 * (1.0 / 120 + t2 * (-1.0 / 5040 + t2 * (1.0 / 362880)))))
    c = 1.0 + t2 * (-0.5 + t2 * (1.0 / 24 + t2 * (-1.0 / 720 + t2 * (1.0 / 40320))))
    quarter = turns.astype(jnp.int32) & 3
    odd = (quarter & 1) == 1
    cosine = jnp.where(odd, s, c)
    sine = jnp.where(odd, c, s)
    cosine = jnp.where((quarter == 1) | (quarter == 2), -cosine, cosine)
    sine = jnp.where(quarter >= 2, -sine, sine)
    return cosine, sine


def spectral_kernel(
    bands, sectors, width, wide, length,
    elevation, velocity, wind, depth, mask, love, numbers,
    out_spec, out_th, out_tl, out_rows, out_cols, out_sine,
    fields, mask_v, x_pad, part, part_in, place_out, place_in, coef, coef_in,
    back_out, back_in, gather_in, row_msg, row_in, col_msg, col_in,
    amu, bee, dee, raw, table_h, table_l,
    load_sem, rs_send, rs_recv, a_send, a_recv, c_send, c_recv,
    s_send, s_recv, g_send, g_recv, h_send, h_recv,
):
    groups = bands // PAIR
    band = lax.axis_index("lat")
    sector = lax.axis_index("lon")
    south = band >= bands // 2
    north_band = jnp.where(south, bands - 1 - band, band)
    group = north_band // 4
    member = jnp.where(south, 7 - north_band % 4, north_band % 4)
    quarter = north_band % 4

    def band_of(g, p):
        n = g * 4 + jnp.where(p >= 4, 7 - p, p)
        return jnp.where(p >= 4, bands - 1 - n, n)

    loads = []
    sources = [
        (mask, mask_v), (elevation.at[0], fields.at[0]), (velocity.at[0, 0], fields.at[1]),
        (velocity.at[0, 1], fields.at[2]), (wind.at[0], fields.at[3]),
        (wind.at[1], fields.at[4]), (depth, fields.at[5]),
    ]
    for i, (src, dst) in enumerate(sources):
        copy = pltpu.make_async_copy(src, dst, load_sem.at[i])
        copy.start()
        loads.append(copy)

    above = ((band + bands - 1) % bands, sector)
    below = ((band + 1) % bands, sector)
    left = (band, (sector + sectors - 1) % sectors)
    right = (band, (sector + 1) % sectors)
    lon_peers = [(band, (sector + d) % sectors) for d in range(1, sectors)]
    group_peers = [(band_of(group, (member + d) % PAIR), sector) for d in range(1, PAIR)]
    wave_peers = [(band_of((group + d) % groups, member), sector) for d in range(1, groups)]
    peers = lon_peers + group_peers + wave_peers + [above, below, left, right]
    barrier = pltpu.get_barrier_semaphore()
    for peer in peers:
        pl.semaphore_signal(barrier, inc=1, device_id=peer, device_id_type=MESH)

    lane = iota((1, 128), 1)
    sub = iota((8, 128), 0)

    def zonal(s, carry):
        waves = jnp.zeros((8, 128), F32)
        for p in range(8):
            waves = jnp.where(sub == p, numbers[s * 8 + p].astype(F32), waves)
        at = pl.multiple_of(s * 16, 16)
        for tile in range(wide // 128):
            t = lane + tile * 128
            column = sector * width + jnp.where(t < width + 16, t, t - wide)
            cosine, sine = circle(waves * column.astype(F32), GRID_LON)
            high, low = halves(jnp.concatenate([cosine, sine], axis=0))
            out_th[pl.ds(at, 16), tile * 128 : tile * 128 + 128] = high
            out_tl[pl.ds(at, 16), tile * 128 : tile * 128 + 128] = low
        return carry

    lax.fori_loop(0, sectors, zonal, 0)

    x_pad[...] = jnp.zeros_like(x_pad)
    loads[0].wait()
    loads[1].wait()
    x_pad[8:56, 0:width] = fields[0] * mask_v[...].astype(F32)
    x_high, x_low = halves(x_pad[...])
    t_high = out_th[...]
    sums = (
        rows_dot_t(t_high, x_high) + rows_dot_t(t_high, x_low) + rows_dot_t(out_tl[...], x_high)
    )
    for s in range(sectors):
        part[s] = sums[16 * s : 16 * s + 16]

    pl.semaphore_wait(barrier, len(peers))
    sends = []

    def send(src, dst, send_sem, recv_sem, peer):
        copy = pltpu.make_async_remote_copy(
            src_ref=src, dst_ref=dst, send_sem=send_sem, recv_sem=recv_sem,
            device_id=peer, device_id_type=MESH,
        )
        copy.start()
        sends.append(copy)
        return copy

    rs = [
        send(part.at[(sector + d) % sectors], part_in.at[d], rs_send.at[d], rs_recv.at[d],
             lon_peers[d - 1])
        for d in range(1, sectors)
    ]

    for i in range(2, 7):
        loads[i].wait()
    wet = mask_v[...].astype(F32)
    row_msg[0, 0:2, :] = fields[0, 0:2, :]
    row_msg[1, 0:2, :] = fields[0, BAND - 2 : BAND, :]
    for slot, index in ((2, 1), (3, 2), (4, 4), (5, 5)):
        row_msg[0, slot : slot + 1, :] = fields[index, 0:1, :]
        row_msg[1, slot : slot + 1, :] = fields[index, BAND - 1 : BAND, :]
    row_msg[0, 6:7, :] = wet[0:1]
    row_msg[1, 6:7, :] = wet[BAND - 1 : BAND]
    for slot, index in ((0, 0), (1, 1), (2, 2), (3, 3), (4, 5)):
        col_msg[0, :, 2 * slot : 2 * slot + 2] = fields[index, :, 0:2]
        col_msg[1, :, 2 * slot : 2 * slot + 2] = fields[index, :, width - 2 : width]
    col_msg[0, :, 10:12] = wet[:, 0:2]
    col_msg[1, :, 10:12] = wet[:, width - 2 : width]
    rims = [
        send(row_msg.at[0], row_in.at[1], h_send.at[0], h_recv.at[0], above),
        send(row_msg.at[1], row_in.at[0], h_send.at[1], h_recv.at[1], below),
        send(col_msg.at[0], col_in.at[1], h_send.at[2], h_recv.at[2], left),
        send(col_msg.at[1], col_in.at[0], h_send.at[3], h_recv.at[3], right),
    ]

    order = numbers[sector * 8 + member].astype(F32)
    lam = iota((1, 256), 1)
    row = group * (4 * BAND) + (lam // SLOT) * BAND - 8 + lam % SLOT
    row_real = row.astype(F32) + 0.5
    cosine, sine = circle(row_real, 2 * GRID_LAT)
    sine = jnp.abs(sine)

    def coefficients(i, carry):
        base = pl.multiple_of(i * 16, 16)
        degree = (base + iota((16, 128), 0)).astype(F32)
        active = degree > order
        gap = jnp.where(active, degree * degree - order * order, 1.0)
        raising = jnp.sqrt((4.0 * degree * degree - 1.0) / gap)
        lower = degree - 1.0
        under = jnp.where(active, lower * lower - order * order, 0.0)
        over = jnp.where(active, 4.0 * lower * lower - 1.0, 1.0)
        lowering = jnp.sqrt(under / over)
        raising = jnp.where(active, raising, 0.0)
        amu[pl.ds(base, 16), 0:128] = raising * cosine[:, 0:128]
        amu[pl.ds(base, 16), 128:256] = raising * cosine[:, 128:256]
        bee[pl.ds(base, 16), :] = raising * lowering
        return carry

    lax.fori_loop(0, length // 16, coefficients, 0)
    first = min(128, length)
    dee[...] = jnp.where(iota((first, 128), 0).astype(F32) == order, 1.0, 0.0)

    ladder = (lane + 1).astype(F32)
    ratio = jnp.where(
        (lane >= 1) & (ladder <= order), jnp.log((2.0 * ladder + 1.0) / (2.0 * ladder)), 0.0
    )
    norm = jnp.sum(ratio, axis=1, keepdims=True) + jnp.where(order > 0.0, math.log(3.0), 0.0)
    log_scale = 0.5 * norm + order * jnp.log(sine)

    def block(inject, i, carry):
        current, previous, scale = carry
        base = pl.multiple_of(i * 16, 16)
        root = jnp.exp(0.5 * scale)
        for t in range(16):
            b = bee[pl.ds(base + t, 1), :]
            rest = jnp.concatenate([b, b], axis=1) * previous
            if inject:
                d = dee[pl.ds(base + t, 1), :]
                rest = rest - jnp.concatenate([d, d], axis=1)
            latest = amu[pl.ds(base + t, 1), :] * current - rest
            raw[t : t + 1, :] = latest
            current, previous = latest, current
        high, low = halves(raw[...] * root * root)
        table_h[pl.ds(base, 16), :] = high
        table_l[pl.ds(base, 16), :] = low
        large = jnp.maximum(jnp.abs(current), jnp.abs(previous)) > 2.0**20
        factor = jnp.where(large, 2.0**-40, 1.0)
        shift = jnp.where(large, 40.0 * math.log(2.0), 0.0)
        return current * factor, previous * factor, scale + shift

    zero = jnp.zeros((1, 256), F32)
    state = lax.fori_loop(
        0, first // 16, functools.partial(block, True), (zero, zero, log_scale)
    )

    for copy in rs:
        copy.wait_recv()
    total = part[sector]
    for d in range(1, sectors):
        total = total + part_in[d]
    slot_row = (band * BAND - 8 + iota((1, SLOT), 1)).astype(F32) + 0.5
    slot_row = jnp.minimum(slot_row, GRID_LAT - slot_row)
    slot_sine = circle(slot_row, 2 * GRID_LAT)[1]
    total = total * (slot_sine * (math.pi / (2.0 * GRID_LAT) / GRID_LON))
    from_row = iota((SLOT, 128), 0)
    to_row = iota((SLOT, 128), 1)
    target = jnp.where(south, SLOT - 1 - from_row, from_row) + SLOT * (quarter % 2)
    move = jnp.where(to_row == target, 1.0, 0.0).astype(BF16)
    high, low = halves(total)
    placed = rows_dot(high, move) + rows_dot(low, move)
    for p in range(PAIR):
        place_out[p, 0:1, :] = placed[p : p + 1]
        place_out[p, 1:2, :] = placed[8 + p : 9 + p]
    place_in[0] = place_out[member]
    moved = [
        send(place_out.at[(member + d) % PAIR], place_in.at[d], a_send.at[d], a_recv.at[d],
             group_peers[d - 1])
        for d in range(1, PAIR)
    ]

    lax.fori_loop(first // 16, length // 16, functools.partial(block, False), state)

    for copy in moved:
        copy.wait_recv()

    def piece(p):
        return place_in[(member + PAIR - p) % PAIR]

    north_rows = jnp.concatenate([piece(0) + piece(1), piece(2) + piece(3)], axis=1)
    south_rows = jnp.concatenate([piece(7) + piece(6), piece(5) + piece(4)], axis=1)
    both = jnp.concatenate([north_rows + south_rows, north_rows - south_rows], axis=0)
    high = both.astype(BF16).astype(F32)
    both = jnp.concatenate([high, both - high], axis=0).astype(BF16)
    product = rows_dot_t(both, table_h[...]) + rows_dot_t(both, table_l[...])
    product = product[0:4] + product[4:8]
    degree = iota((2, length), 1)
    even = (degree + numbers[sector * 8 + member]) % 2 == 0
    coef[...] = jnp.where(even, product[0:2], product[2:4])
    gathered = [
        send(coef, coef_in.at[d], c_send.at[d], c_recv.at[d], wave_peers[d - 1])
        for d in range(1, groups)
    ]
    for copy in gathered:
        copy.wait_recv()
    whole = coef[...]
    for d in range(1, groups):
        whole = whole + coef_in[d]
    whole = whole * (love[...] / (2.0 * iota((1, length), 1).astype(F32) + 1.0))
    split = jnp.concatenate([jnp.where(even, whole, 0.0), jnp.where(even, 0.0, whole)], axis=0)
    high = split.astype(BF16).astype(F32)
    split = jnp.concatenate([high, split - high], axis=0).astype(BF16)
    fields_back = rows_dot(split, table_h[...]) + rows_dot(split, table_l[...])
    fields_back = fields_back[0:4] + fields_back[4:8]
    north_back = fields_back[0:2] + fields_back[2:4]
    south_back = fields_back[0:2] - fields_back[2:4]
    for k in range(2):
        back_out[k] = north_back[:, 128 * k : 128 * k + 128]
        back_out[2 + k] = south_back[:, 128 * k : 128 * k + 128]

    def message(p):
        return jnp.where(p >= 4, 2 + (7 - p) // 2, p // 2)

    back_in[member] = back_out[message(member)]
    returned = []
    for d in range(1, PAIR):
        p = (member + d) % PAIR
        returned.append(
            send(back_out.at[message(p)], back_in.at[member], s_send.at[d], s_recv.at[d],
                 group_peers[d - 1])
        )
    for copy in returned:
        copy.wait_recv()
    gather_in[sector] = back_in[...]
    spread = [
        send(back_in, gather_in.at[sector], g_send.at[d], g_recv.at[d], lon_peers[d - 1])
        for d in range(1, sectors)
    ]

    sub_row = (band * BAND - 8 + iota((SLOT, 128), 0)).astype(F32) + 0.5
    sub_row = jnp.minimum(sub_row, GRID_LAT - sub_row)
    out_sine[...] = circle(sub_row, 2 * GRID_LAT)[1]
    for copy in rims:
        copy.wait_recv()
    out_rows[...] = row_in[...]
    out_cols[...] = col_in[...]
    for copy in spread:
        copy.wait_recv()
    for s in range(sectors):
        for p in range(PAIR):
            for c in range(2):
                at = 16 * s + 8 * c + p
                out_spec[at : at + 1, :] = gather_in[s, p, c : c + 1, :]
    for copy in sends:
        copy.wait_send()


def update_kernel(
    bands, width, wide,
    elevation, velocity, wind, depth, mask, spec, th, tl, rim_rows, rim_cols, sine,
    new_elevation, new_velocity, loading,
    padded, surface, south_flux, loads,
):
    band = lax.axis_index("lat")
    south = band >= bands // 2
    quarter = jnp.where(south, bands - 1 - band, band) % 4

    to_row = iota((SLOT, 128), 0)
    from_row = iota((SLOT, 128), 1)
    source = jnp.where(south, SLOT - 1 - to_row, to_row) + SLOT * (quarter % 2)
    move = jnp.where(from_row == source, 1.0, 0.0).astype(BF16)
    high, low = halves(spec[...])
    high = rows_dot_t(move, high).astype(BF16)
    low = rows_dot_t(move, low).astype(BF16)
    t_high = th[...]
    loads[...] = rows_dot(high, t_high) + rows_dot(low, t_high) + rows_dot(high, tl[...])

    body = slice(8, 8 + BAND)
    padded[0, body, 0:width] = elevation[0]
    padded[1, body, 0:width] = velocity[0, 0]
    padded[2, body, 0:width] = velocity[0, 1]
    padded[3, body, 0:width] = wind[0]
    padded[4, body, 0:width] = wind[1]
    padded[5, body, 0:width] = depth[...]
    padded[6, body, 0:width] = mask[...].astype(F32)
    padded[0, 6:8, 0:width] = rim_rows[0, 0:2, :]
    padded[0, 56:58, 0:width] = rim_rows[1, 0:2, :]
    for slot, index in ((2, 1), (3, 2), (4, 4), (5, 5), (6, 6)):
        padded[index, 7:8, 0:width] = rim_rows[0, slot : slot + 1, :]
        padded[index, 56:57, 0:width] = rim_rows[1, slot : slot + 1, :]
    for slot, index in ((0, 0), (1, 1), (2, 2), (3, 3), (4, 5), (5, 6)):
        padded[index, body, wide - 2 : wide] = rim_cols[0, :, 2 * slot : 2 * slot + 2]
        padded[index, body, width : width + 2] = rim_cols[1, :, 2 * slot : 2 * slot + 2]

    meridional = 0.1 * GRID_LAT / GRID_LON
    sub = iota((8, 1), 0)
    for r in range(8):
        at = slice(8 * r, 8 * r + 8)
        row = band * BAND - 8 + 8 * r + sub
        inside = (row >= 0) & (row < GRID_LAT)
        load = loads[at, :]
        surface[8 + 8 * r : 16 + 8 * r, :] = jnp.where(inside, padded[0, at, :] - load, 0.0)
        if 1 <= r <= 6:
            loading[0, 8 * r - 8 : 8 * r, :] = load[:, 0:width]
    for r in range(8):
        at = slice(8 * r, 8 * r + 8)
        row = band * BAND - 8 + 8 * r + sub
        inside = (row >= 0) & (row < GRID_LAT)
        u = padded[1, at, :]
        v = padded[2, at, :]
        deep = padded[5, at, :]
        inverse = 1.0 / deep
        damping = 1.0 + FRICTION * jnp.sqrt(u * u + v * v) * inverse
        change = surface[9 + 8 * r : 17 + 8 * r, :] - surface[7 + 8 * r : 15 + 8 * r, :]
        new_v = padded[6, at, :] * (v + padded[4, at, :] * inverse - meridional * change) / damping
        flux = sine[at, 0:1] * deep * new_v
        south_flux[at, :] = jnp.where(inside, flux, 0.0)
        if 1 <= r <= 6:
            new_velocity[0, 1, 8 * r - 8 : 8 * r, :] = new_v[:, 0:width]
    for r in range(1, 7):
        at = slice(8 * r, 8 * r + 8)
        u = padded[1, at, :]
        v = padded[2, at, :]
        deep = padded[5, at, :]
        wet = padded[6, at, :]
        inverse = 1.0 / deep
        damping = 1.0 + FRICTION * jnp.sqrt(u * u + v * v) * inverse
        here = surface[8 + 8 * r : 16 + 8 * r, :]
        change = pltpu.roll(here, wide - 1, 1) - pltpu.roll(here, 1, 1)
        row_sine = sine[at, 0:1]
        zonal = STEP_RATIO / row_sine
        new_u = wet * (u + padded[3, at, :] * inverse - zonal * change) / damping
        flux = deep * new_u
        east = pltpu.roll(flux, wide - 1, 1) - pltpu.roll(flux, 1, 1)
        down = south_flux[8 * r + 1 : 8 * r + 9, :] - south_flux[8 * r - 1 : 8 * r + 7, :]
        tendency = zonal * east + (meridional / row_sine) * down
        level = padded[0, at, :] - wet * tendency
        new_velocity[0, 0, 8 * r - 8 : 8 * r, :] = new_u[:, 0:width]
        new_elevation[0, 8 * r - 8 : 8 * r, :] = level[:, 0:width]


def local(bands, sectors, elevation, velocity, wind_forcing, ocean_depth, wet_mask, love_factor,
          wavenumbers):
    width = elevation.shape[2]
    wide = -(-(width + 18) // 128) * 128
    length = -(-DEGREES // 16) * 16
    groups = bands // PAIR
    love = jnp.pad(love_factor, (0, length - DEGREES)).reshape(1, length)
    vmem = pl.BlockSpec(memory_space=pltpu.VMEM)
    hbm = pl.BlockSpec(memory_space=pl.ANY)
    smem = pl.BlockSpec(memory_space=pltpu.SMEM)
    dma = pltpu.SemaphoreType.DMA
    spec, th, tl, rim_rows, rim_cols, sine = pl.pallas_call(
        functools.partial(spectral_kernel, bands, sectors, width, wide, length),
        out_shape=[
            jax.ShapeDtypeStruct((16 * sectors, 128), F32),
            jax.ShapeDtypeStruct((16 * sectors, wide), BF16),
            jax.ShapeDtypeStruct((16 * sectors, wide), BF16),
            jax.ShapeDtypeStruct((2, 8, width), F32),
            jax.ShapeDtypeStruct((2, BAND, 128), F32),
            jax.ShapeDtypeStruct((SLOT, 128), F32),
        ],
        in_specs=[hbm] * 5 + [vmem, smem],
        out_specs=[vmem] * 6,
        scratch_shapes=[
            pltpu.VMEM((6, BAND, width), F32),
            pltpu.VMEM((BAND, width), jnp.int32),
            pltpu.VMEM((SLOT, wide), F32),
            pltpu.VMEM((sectors, 16, SLOT), F32),
            pltpu.VMEM((sectors, 16, SLOT), F32),
            pltpu.VMEM((PAIR, 2, 128), F32),
            pltpu.VMEM((PAIR, 2, 128), F32),
            pltpu.VMEM((2, length), F32),
            pltpu.VMEM((groups, 2, length), F32),
            pltpu.VMEM((4, 2, 128), F32),
            pltpu.VMEM((PAIR, 2, 128), F32),
            pltpu.VMEM((sectors, PAIR, 2, 128), F32),
            pltpu.VMEM((2, 8, width), F32),
            pltpu.VMEM((2, 8, width), F32),
            pltpu.VMEM((2, BAND, 128), F32),
            pltpu.VMEM((2, BAND, 128), F32),
            pltpu.VMEM((length, 256), F32),
            pltpu.VMEM((length, 128), F32),
            pltpu.VMEM((min(128, length), 128), F32),
            pltpu.VMEM((16, 256), F32),
            pltpu.VMEM((length, 256), BF16),
            pltpu.VMEM((length, 256), BF16),
            dma((7,)),
            dma((sectors,)), dma((sectors,)),
            dma((PAIR,)), dma((PAIR,)),
            dma((groups,)), dma((groups,)),
            dma((PAIR,)), dma((PAIR,)),
            dma((sectors,)), dma((sectors,)),
            dma((4,)), dma((4,)),
        ],
        compiler_params=pltpu.CompilerParams(
            collective_id=0, has_side_effects=True, vmem_limit_bytes=24 * 1024 * 1024
        ),
        name="spectral",
    )(elevation, velocity, wind_forcing, ocean_depth, wet_mask, love, wavenumbers)
    return pl.pallas_call(
        functools.partial(update_kernel, bands, width, wide),
        out_shape=[
            jax.ShapeDtypeStruct(elevation.shape, F32),
            jax.ShapeDtypeStruct(velocity.shape, F32),
            jax.ShapeDtypeStruct(elevation.shape, F32),
        ],
        in_specs=[vmem] * 11,
        out_specs=[vmem] * 3,
        scratch_shapes=[
            pltpu.VMEM((7, SLOT, wide), F32),
            pltpu.VMEM((SLOT + 16, wide), F32),
            pltpu.VMEM((SLOT, wide), F32),
            pltpu.VMEM((SLOT, wide), F32),
        ],
        compiler_params=pltpu.CompilerParams(vmem_limit_bytes=24 * 1024 * 1024),
        name="update",
    )(elevation, velocity, wind_forcing, ocean_depth, wet_mask, spec, th, tl, rim_rows, rim_cols,
      sine)


def solution(mesh):
    bands, sectors = mesh.shape["lat"], mesh.shape["lon"]
    return jax.shard_map(
        functools.partial(local, bands, sectors),
        mesh=mesh,
        in_specs=(
            P(None, "lat", "lon"),
            P(None, None, "lat", "lon"),
            P(None, "lat", "lon"),
            P("lat", "lon"),
            P("lat", "lon"),
            P(),
            P(),
        ),
        out_specs=(P(None, "lat", "lon"), P(None, None, "lat", "lon"), P(None, "lat", "lon")),
        check_vma=False,
    )
```

```python
import functools
import math

import jax
import jax.numpy as jnp
from jax import lax
from jax.experimental import pallas as pl
from jax.experimental.pallas import tpu as pltpu
from jax.sharding import PartitionSpec as P

GRID_LAT = 3072
GRID_LON = 8640
DEGREES = 1081
STEP_RATIO = 0.05
FRICTION = 0.1

BAND = 48
SLOT = 64
PILE = 8
F32 = jnp.float32
BF16 = jnp.bfloat16
MESH = pl.DeviceIdType.MESH
HBM = pltpu.MemorySpace.HBM
SPLIT = 44


def iota(shape, dim):
    return lax.broadcasted_iota(jnp.int32, shape, dim)


def halves(x):
    high = x.astype(BF16)
    return high, (x - high.astype(F32)).astype(BF16)


def rows_dot(a, b):
    return lax.dot_general(a, b, (((1,), (0,)), ((), ())), preferred_element_type=F32)


def rows_dot_t(a, b):
    return lax.dot_general(a, b, (((1,), (1,)), ((), ())), preferred_element_type=F32)


def circle(phase, period):
    turns = jnp.floor(phase * (4.0 / period) + 0.5)
    t = (phase - turns * (period / 4.0)) * (2.0 * math.pi / period)
    t2 = t * t
    s = t * (1.0 + t2 * (-1.0 / 6 + t2 * (1.0 / 120 + t2 * (-1.0 / 5040 + t2 * (1.0 / 362880)))))
    c = 1.0 + t2 * (-0.5 + t2 * (1.0 / 24 + t2 * (-1.0 / 720 + t2 * (1.0 / 40320))))
    quarter = turns.astype(jnp.int32) & 3
    odd = (quarter & 1) == 1
    cosine = jnp.where(odd, s, c)
    sine = jnp.where(odd, c, s)
    cosine = jnp.where((quarter == 1) | (quarter == 2), -cosine, cosine)
    sine = jnp.where(quarter >= 2, -sine, sine)
    return cosine, sine


def spectral_kernel(
    bands, sectors, width, wide, length,
    elevation, velocity, wind, depth, mask, love, waves_hbm,
    out_spec, out_th, out_tl, out_fields, out_sine,
    numbers, fields, mask_v, love_v, x_pad, part, part_in, place_out, place_in, coef, coef_in,
    back_out, back_in, ring_out, row_msg, row_in, col_msg, col_in,
    ladder_v, ladder_s, raw, table_h, table_l, spec_in,
    load_sem, rs_send, rs_recv, a_send, a_recv, c_send, c_recv,
    s_send, s_recv, g_send, g_recv, h_send, h_recv,
):
    depths = bands // PILE
    ring = 2 * sectors
    band = lax.axis_index("lat")
    sector = lax.axis_index("lon")
    z, x, half = band // 8, (band // 2) % 4, band % 2
    place = half * sectors + sector

    sources = [
        (waves_hbm, numbers), (mask, mask_v), (elevation.at[0], fields.at[0]), (love, love_v),
        (velocity.at[0, 0], fields.at[1]), (velocity.at[0, 1], fields.at[2]),
        (wind.at[0], fields.at[3]), (wind.at[1], fields.at[4]), (depth, fields.at[5]),
    ]
    loads = [pltpu.make_async_copy(a, b, load_sem.at[i]) for i, (a, b) in enumerate(sources)]
    for copy in loads:
        copy.start()

    above = ((band + bands - 1) % bands, sector)
    below = ((band + 1) % bands, sector)
    left = (band, (sector + sectors - 1) % sectors)
    right = (band, (sector + 1) % sectors)

    def ring_peer(t):
        return (z * 8 + x * 2 + t // sectors, t % sectors)

    ring_peers = [ring_peer((place + d) % ring) for d in range(1, ring)]
    x_peers = [(z * 8 + ((x + d) % 4) * 2 + half, sector) for d in range(1, 4)]
    z_peers = [(((z + d) % depths) * 8 + x * 2 + half, sector) for d in range(1, depths)]
    peers = ring_peers + x_peers + z_peers + [above, below, left, right]
    barrier = pltpu.get_barrier_semaphore()
    for peer in peers:
        pl.semaphore_signal(barrier, inc=1, device_id=peer, device_id_type=MESH)

    loads[0].wait()

    lane = iota((1, 128), 1)
    sub = iota((8, 128), 0)

    def zonal(s, carry):
        waves = jnp.zeros((8, 128), F32)
        for p in range(8):
            waves = jnp.where(sub == p, numbers[s * 8 + p].astype(F32), waves)
        at = pl.multiple_of(s * 16, 16)
        for tile in range(wide // 128):
            t = lane + tile * 128
            column = sector * width + jnp.where(t < width + 16, t, t - wide)
            cosine, sine = circle(waves * column.astype(F32), GRID_LON)
            high, low = halves(
                jnp.concatenate([cosine[0:4], sine[0:4], cosine[4:8], sine[4:8]], axis=0)
            )
            out_th[pl.ds(at, 16), tile * 128 : tile * 128 + 128] = high
            out_tl[pl.ds(at, 16), tile * 128 : tile * 128 + 128] = low
        return carry

    lax.fori_loop(0, sectors, zonal, 0)

    x_pad[...] = jnp.zeros_like(x_pad)
    loads[1].wait()
    loads[2].wait()
    x_pad[8:56, 0:width] = fields[0] * mask_v[...].astype(F32)
    x_high, x_low = halves(x_pad[...])
    t_high = out_th[...]
    sums = (
        rows_dot_t(t_high, x_high) + rows_dot_t(t_high, x_low) + rows_dot_t(out_tl[...], x_high)
    )
    for t in range(ring):
        part[t] = sums[8 * t : 8 * t + 8]

    number = numbers[place * 4 + x]
    order = number.astype(F32)
    degree = (iota((16, 128), 0) * 128 + iota((16, 128), 1)).astype(F32)
    active = degree > order
    gap = jnp.where(active, degree * degree - order * order, 1.0)
    raising = jnp.sqrt((4.0 * degree * degree - 1.0) / gap)
    lower = degree - 1.0
    under = jnp.where(active, lower * lower - order * order, 0.0)
    over = jnp.where(active, 4.0 * lower * lower - 1.0, 1.0)
    raising = jnp.where(active, raising, 0.0)
    ladder_v[0:16, :] = raising
    ladder_v[16:32, :] = raising * jnp.sqrt(under / over)
    to_scalar = pltpu.make_async_copy(ladder_v, ladder_s, load_sem.at[len(sources)])
    to_scalar.start()

    pl.semaphore_wait(barrier, len(peers))
    sends = []

    def send(src, dst, send_sem, recv_sem, peer):
        copy = pltpu.make_async_remote_copy(
            src_ref=src, dst_ref=dst, send_sem=send_sem, recv_sem=recv_sem,
            device_id=peer, device_id_type=MESH,
        )
        copy.start()
        sends.append(copy)
        return copy

    rs = [
        send(part.at[(place + d) % ring], part_in.at[place], rs_send.at[d], rs_recv.at[d],
             ring_peers[d - 1])
        for d in range(1, ring)
    ]
    part_in[place] = part[place]

    for i in range(3, len(sources)):
        loads[i].wait()
    wet = mask_v[...].astype(F32)
    row_msg[0, 0:2, :] = fields[0, 0:2, :]
    row_msg[1, 0:2, :] = fields[0, BAND - 2 : BAND, :]
    for slot, index in ((2, 1), (3, 2), (4, 4), (5, 5)):
        row_msg[0, slot : slot + 1, :] = fields[index, 0:1, :]
        row_msg[1, slot : slot + 1, :] = fields[index, BAND - 1 : BAND, :]
    row_msg[0, 6:7, :] = wet[0:1]
    row_msg[1, 6:7, :] = wet[BAND - 1 : BAND]
    for slot, index in ((0, 0), (1, 1), (2, 2), (3, 3), (4, 5)):
        col_msg[0, :, 2 * slot : 2 * slot + 2] = fields[index, :, 0:2]
        col_msg[1, :, 2 * slot : 2 * slot + 2] = fields[index, :, width - 2 : width]
    col_msg[0, :, 10:12] = wet[:, 0:2]
    col_msg[1, :, 10:12] = wet[:, width - 2 : width]
    rims = [
        send(row_msg.at[0], row_in.at[1], h_send.at[0], h_recv.at[0], above),
        send(row_msg.at[1], row_in.at[0], h_send.at[1], h_recv.at[1], below),
        send(col_msg.at[0], col_in.at[1], h_send.at[2], h_recv.at[2], left),
        send(col_msg.at[1], col_in.at[0], h_send.at[3], h_recv.at[3], right),
    ]

    row = (z * 8 + 2 * iota((4, 128), 0) + iota((4, 128), 1) // SLOT) * BAND - 8
    row = row + iota((4, 128), 1) % SLOT
    cosine, sine = circle(row.astype(F32) + 0.5, 2 * GRID_LAT)
    ladder = (lane + 1).astype(F32)
    ratio = jnp.where(
        (lane >= 1) & (ladder <= order), jnp.log((2.0 * ladder + 1.0) / (2.0 * ladder)), 0.0
    )
    norm = jnp.sum(ratio, axis=1, keepdims=True) + jnp.where(order > 0.0, math.log(3.0), 0.0)
    log_scale = 0.5 * norm + order * jnp.log(jnp.abs(sine))
    to_scalar.wait()

    def block(inject, i, carry):
        current, previous, scale = carry
        base = pl.multiple_of(i * 16, 16)
        line, first = i // 8, (i % 8) * 16
        root = jnp.exp(0.5 * scale)
        for t in range(16):
            rest = ladder_s[16 + line, first + t] * previous
            if inject:
                rest = rest - jnp.where(base + t == number, 1.0, 0.0)
            latest = (ladder_s[line, first + t] * cosine) * current - rest
            raw[4 * t : 4 * t + 4, :] = latest
            current, previous = latest, current
        for k in range(4):
            factor = root[k : k + 1]
            high, low = halves(raw[pl.ds(k, 16, stride=4), :] * factor * factor)
            table_h[pl.ds(base, 16), 128 * k : 128 * k + 128] = high
            table_l[pl.ds(base, 16), 128 * k : 128 * k + 128] = low
        large = jnp.maximum(jnp.abs(current), jnp.abs(previous)) > 2.0**20
        factor = jnp.where(large, 2.0**-40, 1.0)
        shift = jnp.where(large, 40.0 * math.log(2.0), 0.0)
        return current * factor, previous * factor, scale + shift

    zero = jnp.zeros((4, 128), F32)
    blocks = length // 16
    early = min(8, blocks)
    middle = min(SPLIT, blocks)
    state = (zero, zero, log_scale)
    state = lax.fori_loop(0, early, functools.partial(block, True), state)
    state = lax.fori_loop(early, middle, functools.partial(block, False), state)

    for copy in rs:
        copy.wait_recv()
    pieces = []
    for h in range(2):
        total = part_in[h * sectors]
        for s in range(1, sectors):
            total = total + part_in[h * sectors + s]
        pieces.append(total)
    total = jnp.concatenate(pieces, axis=1)
    slot_row = (z * 8 + x * 2 + lane // SLOT) * BAND - 8 + lane % SLOT
    slot_sine = circle(slot_row.astype(F32) + 0.5, 2 * GRID_LAT)[1]
    total = total * (slot_sine * (math.pi / (2.0 * GRID_LAT) / GRID_LON))
    for p in range(4):
        place_out[p, 0:1, :] = total[p : p + 1]
        place_out[p, 1:2, :] = total[4 + p : 5 + p]
    moved = [
        send(place_out.at[(x + d) % 4], place_in.at[x], a_send.at[d], a_recv.at[d],
             x_peers[d - 1])
        for d in range(1, 4)
    ]
    place_in[x] = place_out[x]

    lax.fori_loop(middle, blocks, functools.partial(block, False), state)

    for copy in moved:
        copy.wait_recv()
    rows = jnp.concatenate([place_in[k] for k in range(4)], axis=1)
    high = rows.astype(BF16).astype(F32)
    rows = jnp.concatenate([high, rows - high], axis=0).astype(BF16)
    product = rows_dot_t(rows, table_h[...]) + rows_dot_t(rows, table_l[...])
    coef[...] = product[0:2] + product[2:4]
    gathered = [
        send(coef, coef_in.at[d], c_send.at[d], c_recv.at[d], z_peers[d - 1])
        for d in range(1, depths)
    ]

    for copy in rims:
        copy.wait_recv()
    sub_row = band * BAND - 8 + iota((SLOT, 128), 0)
    band_sine = circle(sub_row.astype(F32) + 0.5, 2 * GRID_LAT)[1]
    out_sine[...] = band_sine
    body = slice(8, 8 + BAND)
    for index in range(6):
        out_fields[index, body, 0:width] = fields[index]
    out_fields[6, body, 0:width] = wet
    out_fields[0, 6:8, 0:width] = row_in[0, 0:2, :]
    out_fields[0, 56:58, 0:width] = row_in[1, 0:2, :]
    for slot, index in ((2, 1), (3, 2), (4, 4), (5, 5), (6, 6)):
        out_fields[index, 7:8, 0:width] = row_in[0, slot : slot + 1, :]
        out_fields[index, 56:57, 0:width] = row_in[1, slot : slot + 1, :]
    for slot, index in ((0, 0), (1, 1), (2, 2), (3, 3), (4, 5), (5, 6)):
        out_fields[index, body, wide - 2 : wide] = col_in[0, :, 2 * slot : 2 * slot + 2]
        out_fields[index, body, width : width + 2] = col_in[1, :, 2 * slot : 2 * slot + 2]
    meridional = 0.1 * GRID_LAT / GRID_LON

    def prepare(r, carry):
        at = pl.ds(pl.multiple_of(8 * r, 8), 8)
        u = out_fields[1, at, :]
        v = out_fields[2, at, :]
        inverse = 1.0 / out_fields[5, at, :]
        damping = 1.0 + FRICTION * jnp.sqrt(u * u + v * v) * inverse
        share = out_fields[6, at, :] / damping
        zonal_step = STEP_RATIO / out_sine[at, 0:1]
        out_fields[1, at, :] = share * (u + out_fields[3, at, :] * inverse)
        out_fields[2, at, :] = share * zonal_step
        out_fields[3, at, :] = share * (v + out_fields[4, at, :] * inverse)
        out_fields[4, at, :] = share * meridional
        return carry

    lax.fori_loop(0, SLOT // 8, prepare, 0)

    for copy in gathered:
        copy.wait_recv()
    whole = coef[...]
    for d in range(1, depths):
        whole = whole + coef_in[d]
    degrees = love_v.shape[1]
    weight = love_v[...] / (2.0 * iota((1, degrees), 1).astype(F32) + 1.0)
    weight = jnp.concatenate([weight, jnp.zeros((1, length - degrees), F32)], axis=1)
    whole = whole * weight
    high = whole.astype(BF16).astype(F32)
    whole = jnp.concatenate([high, whole - high], axis=0).astype(BF16)
    product = rows_dot(whole, table_h[...]) + rows_dot(whole, table_l[...])
    product = product[0:2] + product[2:4]
    for k in range(4):
        back_out[k] = product[:, 128 * k : 128 * k + 128]
    returned = [
        send(back_out.at[(x + d) % 4], back_in.at[x], s_send.at[d], s_recv.at[d], x_peers[d - 1])
        for d in range(1, 4)
    ]
    back_in[x] = back_out[x]
    for copy in returned:
        copy.wait_recv()
    for k in range(4):
        ring_out[k : k + 1, :] = back_in[k, 0:1, :]
        ring_out[4 + k : 5 + k, :] = back_in[k, 1:2, :]
    spread = [
        send(ring_out, spec_in.at[place], g_send.at[d], g_recv.at[d], ring_peers[d - 1])
        for d in range(1, ring)
    ]
    spec_in[place] = ring_out[...]
    for copy in spread:
        copy.wait_recv()
    out_spec[...] = spec_in[...]
    for copy in sends:
        copy.wait_send()


def update_kernel(
    bands, width, wide,
    spec, th, tl, fields, sine,
    new_elevation, new_velocity, loading,
    surface, south_flux, loads,
):
    band = lax.axis_index("lat")

    source = iota((SLOT, 128), 0) + SLOT * (band % 2)
    move = jnp.where(iota((SLOT, 128), 1) == source, 1.0, 0.0).astype(BF16)
    high, low = halves(spec[...].reshape(th.shape[0], 128))
    high = rows_dot_t(move, high).astype(BF16)
    low = rows_dot_t(move, low).astype(BF16)
    t_high = th[...]
    loads[...] = rows_dot(high, t_high) + rows_dot(low, t_high) + rows_dot(high, tl[...])

    meridional = 0.1 * GRID_LAT / GRID_LON
    sub = iota((8, 1), 0)
    for r in range(8):
        at = slice(8 * r, 8 * r + 8)
        row = band * BAND - 8 + 8 * r + sub
        inside = (row >= 0) & (row < GRID_LAT)
        load = loads[at, :]
        surface[8 + 8 * r : 16 + 8 * r, :] = jnp.where(inside, fields[0, at, :] - load, 0.0)
        if 1 <= r <= 6:
            loading[0, 8 * r - 8 : 8 * r, :] = load[:, 0:width]
    for r in range(8):
        at = slice(8 * r, 8 * r + 8)
        row = band * BAND - 8 + 8 * r + sub
        inside = (row >= 0) & (row < GRID_LAT)
        change = surface[9 + 8 * r : 17 + 8 * r, :] - surface[7 + 8 * r : 15 + 8 * r, :]
        new_v = fields[3, at, :] - fields[4, at, :] * change
        flux = sine[at, 0:1] * fields[5, at, :] * new_v
        south_flux[at, :] = jnp.where(inside, flux, 0.0)
        if 1 <= r <= 6:
            new_velocity[0, 1, 8 * r - 8 : 8 * r, :] = new_v[:, 0:width]
    for r in range(1, 7):
        at = slice(8 * r, 8 * r + 8)
        here = surface[8 + 8 * r : 16 + 8 * r, :]
        change = pltpu.roll(here, wide - 1, 1) - pltpu.roll(here, 1, 1)
        new_u = fields[1, at, :] - fields[2, at, :] * change
        flux = fields[5, at, :] * new_u
        east = pltpu.roll(flux, wide - 1, 1) - pltpu.roll(flux, 1, 1)
        down = south_flux[8 * r + 1 : 8 * r + 9, :] - south_flux[8 * r - 1 : 8 * r + 7, :]
        row_sine = sine[at, 0:1]
        tendency = (STEP_RATIO / row_sine) * east + (meridional / row_sine) * down
        level = fields[0, at, :] - fields[6, at, :] * tendency
        new_velocity[0, 0, 8 * r - 8 : 8 * r, :] = new_u[:, 0:width]
        new_elevation[0, 8 * r - 8 : 8 * r, :] = level[:, 0:width]


def local(bands, sectors, elevation, velocity, wind_forcing, ocean_depth, wet_mask, love_factor,
          wavenumbers):
    width = elevation.shape[2]
    wide = -(-(width + 18) // 128) * 128
    length = -(-DEGREES // 16) * 16
    depths = bands // PILE
    ring = 2 * sectors
    vmem = pl.BlockSpec(memory_space=pltpu.VMEM)
    hbm = pl.BlockSpec(memory_space=HBM)
    dma = pltpu.SemaphoreType.DMA
    shared = pl.pallas_call(
        functools.partial(spectral_kernel, bands, sectors, width, wide, length),
        out_shape=[
            jax.ShapeDtypeStruct((ring, 8, 128), F32),
            jax.ShapeDtypeStruct((8 * ring, wide), BF16),
            jax.ShapeDtypeStruct((8 * ring, wide), BF16),
            jax.ShapeDtypeStruct((7, SLOT, wide), F32),
            jax.ShapeDtypeStruct((SLOT, 128), F32),
        ],
        in_specs=[hbm] * 7,
        out_specs=[vmem] * 5,
        scratch_shapes=[
            pltpu.SMEM((8 * sectors,), jnp.int32),
            pltpu.VMEM((6, BAND, width), F32),
            pltpu.VMEM((BAND, width), jnp.int32),
            pltpu.VMEM((1, DEGREES), F32),
            pltpu.VMEM((SLOT, wide), F32),
            pltpu.VMEM((ring, 8, SLOT), F32),
            pltpu.VMEM((ring, 8, SLOT), F32),
            pltpu.VMEM((4, 2, 128), F32),
            pltpu.VMEM((4, 2, 128), F32),
            pltpu.VMEM((2, length), F32),
            pltpu.VMEM((depths, 2, length), F32),
            pltpu.VMEM((4, 2, 128), F32),
            pltpu.VMEM((4, 2, 128), F32),
            pltpu.VMEM((8, 128), F32),
            pltpu.VMEM((2, 8, width), F32),
            pltpu.VMEM((2, 8, width), F32),
            pltpu.VMEM((2, BAND, 128), F32),
            pltpu.VMEM((2, BAND, 128), F32),
            pltpu.VMEM((32, 128), F32),
            pltpu.SMEM((32, 128), F32),
            pltpu.VMEM((64, 128), F32),
            pltpu.VMEM((length, 512), BF16),
            pltpu.VMEM((length, 512), BF16),
            pltpu.VMEM((ring, 8, 128), F32),
            dma((10,)),
            dma((ring,)), dma((ring,)),
            dma((4,)), dma((4,)),
            dma((depths,)), dma((depths,)),
            dma((4,)), dma((4,)),
            dma((ring,)), dma((ring,)),
            dma((4,)), dma((4,)),
        ],
        compiler_params=pltpu.CompilerParams(
            collective_id=0, has_side_effects=True, vmem_limit_bytes=24 * 1024 * 1024
        ),
        name="spectral",
    )(*[
        pltpu.with_memory_space_constraint(array, HBM)
        for array in (elevation, velocity, wind_forcing, ocean_depth, wet_mask,
                      love_factor.reshape(1, DEGREES), wavenumbers)
    ])
    return pl.pallas_call(
        functools.partial(update_kernel, bands, width, wide),
        out_shape=[
            jax.ShapeDtypeStruct(elevation.shape, F32),
            jax.ShapeDtypeStruct(velocity.shape, F32),
            jax.ShapeDtypeStruct(elevation.shape, F32),
        ],
        in_specs=[vmem] * 5,
        out_specs=[vmem] * 3,
        scratch_shapes=[
            pltpu.VMEM((SLOT + 16, wide), F32),
            pltpu.VMEM((SLOT, wide), F32),
            pltpu.VMEM((SLOT, wide), F32),
        ],
        compiler_params=pltpu.CompilerParams(vmem_limit_bytes=24 * 1024 * 1024),
        name="update",
    )(*shared)


def solution(mesh):
    bands, sectors = mesh.shape["lat"], mesh.shape["lon"]
    return jax.shard_map(
        functools.partial(local, bands, sectors),
        mesh=mesh,
        in_specs=(
            P(None, "lat", "lon"),
            P(None, None, "lat", "lon"),
            P(None, "lat", "lon"),
            P("lat", "lon"),
            P("lat", "lon"),
            P(),
            P(),
        ),
        out_specs=(P(None, "lat", "lon"), P(None, None, "lat", "lon"), P(None, "lat", "lon")),
        check_vma=False,
    )
```

```python
import functools
import math

import jax
import jax.numpy as jnp
from jax import lax
from jax.experimental import pallas as pl
from jax.experimental.pallas import tpu as pltpu
from jax.sharding import PartitionSpec as P

GRID_LAT = 3072
GRID_LON = 8640
DEGREES = 1081
STEP_RATIO = 0.05
FRICTION = 0.1

BAND = 48
SLOT = 64
PILE = 8
F32 = jnp.float32
BF16 = jnp.bfloat16
MESH = pl.DeviceIdType.MESH
HBM = pltpu.MemorySpace.HBM


def iota(shape, dim):
    return lax.broadcasted_iota(jnp.int32, shape, dim)


def halves(x):
    high = x.astype(BF16)
    return high, (x - high.astype(F32)).astype(BF16)


def rows_dot(a, b):
    return lax.dot_general(a, b, (((1,), (0,)), ((), ())), preferred_element_type=F32)


def rows_dot_t(a, b):
    return lax.dot_general(a, b, (((1,), (1,)), ((), ())), preferred_element_type=F32)


def circle(phase, period):
    turns = jnp.floor(phase * (4.0 / period) + 0.5)
    t = (phase - turns * (period / 4.0)) * (2.0 * math.pi / period)
    t2 = t * t
    s = t * (1.0 + t2 * (-1.0 / 6 + t2 * (1.0 / 120 + t2 * (-1.0 / 5040 + t2 * (1.0 / 362880)))))
    c = 1.0 + t2 * (-0.5 + t2 * (1.0 / 24 + t2 * (-1.0 / 720 + t2 * (1.0 / 40320))))
    quarter = turns.astype(jnp.int32) & 3
    odd = (quarter & 1) == 1
    cosine = jnp.where(odd, s, c)
    sine = jnp.where(odd, c, s)
    cosine = jnp.where((quarter == 1) | (quarter == 2), -cosine, cosine)
    sine = jnp.where(quarter >= 2, -sine, sine)
    return cosine, sine


def spectral_kernel(
    bands, sectors, width, wide, length,
    elevation, velocity, wind, depth, mask, love, waves_hbm,
    out_spec, out_th, out_tl, out_fields, out_sine,
    numbers, fields, mask_v, love_v, x_pad, part, pair_in, mine, piece_in, coef, coef_in,
    back_out, row_msg, row_in, col_msg, col_in,
    ladder_v, ladder_s, raw, table_h, table_l, spec_in,
    load_sem, pair_send, pair_recv, a_send, a_recv, c_send, c_recv,
    s_send, s_recv, last_send, last_recv, h_send, h_recv,
):
    depths = bands // PILE
    lows = sectors // 2
    share = 4 * sectors
    band = lax.axis_index("lat")
    sector = lax.axis_index("lon")
    z, x, half = band // 8, (band // 2) % 4, band % 2
    low, core = sector // 2, sector % 2
    place = (half * lows + low) * 4 + x

    sources = [
        (waves_hbm, numbers), (mask, mask_v), (elevation.at[0], fields.at[0]), (love, love_v),
        (velocity.at[0, 0], fields.at[1]), (velocity.at[0, 1], fields.at[2]),
        (wind.at[0], fields.at[3]), (wind.at[1], fields.at[4]), (depth, fields.at[5]),
    ]
    loads = [pltpu.make_async_copy(a, b, load_sem.at[i]) for i, (a, b) in enumerate(sources)]
    for copy in loads:
        copy.start()

    above = ((band + bands - 1) % bands, sector)
    below = ((band + 1) % bands, sector)
    left = (band, (sector + sectors - 1) % sectors)
    right = (band, (sector + 1) % sectors)

    def chip(t):
        y = t // 4
        return (z * 8 + (t % 4) * 2 + y // lows, (y % lows) * 2 + core)

    partner = (band, low * 2 + 1 - core)
    chips = [chip((place + d) % share) for d in range(1, share)]
    z_peers = [(((z + d) % depths) * 8 + x * 2 + half, sector) for d in range(1, depths)]
    peers = [partner] + chips + z_peers + [above, below, left, right]
    barrier = pltpu.get_barrier_semaphore()
    for peer in peers:
        pl.semaphore_signal(barrier, inc=1, device_id=peer, device_id_type=MESH)

    loads[0].wait()

    lane = iota((1, 128), 1)
    sub = iota((16, 128), 0)

    def zonal(s, carry):
        waves = jnp.zeros((16, 128), F32)
        for p in range(16):
            waves = jnp.where(sub == p, numbers[s * 16 + p].astype(F32), waves)
        at = pl.multiple_of((s // (share // 16)) * 2 * share + (s % (share // 16)) * 16, 16)
        for tile in range(wide // 128):
            t = lane + tile * 128
            column = sector * width + jnp.where(t < width + 16, t, t - wide)
            cosine, sine = circle(waves * column.astype(F32), GRID_LON)
            high, low_part = halves(cosine)
            out_th[pl.ds(at, 16), tile * 128 : tile * 128 + 128] = high
            out_tl[pl.ds(at, 16), tile * 128 : tile * 128 + 128] = low_part
            high, low_part = halves(sine)
            out_th[pl.ds(at + share, 16), tile * 128 : tile * 128 + 128] = high
            out_tl[pl.ds(at + share, 16), tile * 128 : tile * 128 + 128] = low_part
        return carry

    lax.fori_loop(0, share // 8, zonal, 0)

    x_pad[...] = jnp.zeros_like(x_pad)
    loads[1].wait()
    loads[2].wait()
    x_pad[8:56, 0:width] = fields[0] * mask_v[...].astype(F32)
    x_high, x_low = halves(x_pad[...])
    t_high = out_th[...]
    sums = (
        rows_dot_t(t_high, x_high) + rows_dot_t(t_high, x_low) + rows_dot_t(out_tl[...], x_high)
    )
    part[0] = sums[0 : 2 * share]
    part[1] = sums[2 * share : 4 * share]

    pl.semaphore_wait(barrier, len(peers))
    sends = []

    def send(src, dst, send_sem, recv_sem, peer):
        copy = pltpu.make_async_remote_copy(
            src_ref=src, dst_ref=dst, send_sem=send_sem, recv_sem=recv_sem,
            device_id=peer, device_id_type=MESH,
        )
        copy.start()
        sends.append(copy)
        return copy

    pair = send(part.at[1 - core], pair_in, pair_send.at[0], pair_recv.at[0], partner)

    number = numbers[core * share + place]
    order = number.astype(F32)
    degree = (iota((16, 128), 0) * 128 + iota((16, 128), 1)).astype(F32)
    active = degree > order
    gap = jnp.where(active, degree * degree - order * order, 1.0)
    raising = jnp.sqrt((4.0 * degree * degree - 1.0) / gap)
    lower = degree - 1.0
    under = jnp.where(active, lower * lower - order * order, 0.0)
    over = jnp.where(active, 4.0 * lower * lower - 1.0, 1.0)
    raising = jnp.where(active, raising, 0.0)
    ladder_v[0:16, :] = raising
    ladder_v[16:32, :] = raising * jnp.sqrt(under / over)
    to_scalar = pltpu.make_async_copy(ladder_v, ladder_s, load_sem.at[len(sources)])
    to_scalar.start()

    slot_row = band * BAND - 8 + iota((1, SLOT), 1)
    slot_sine = circle(slot_row.astype(F32) + 0.5, 2 * GRID_LAT)[1]
    weights = slot_sine * (math.pi / (2.0 * GRID_LAT) / GRID_LON)
    own = part[core]
    pair.wait_recv()
    total = (own + pair_in[...]) * weights
    mine[0] = total[0:share]
    mine[1] = total[share : 2 * share]
    slot = 2 * x + half
    moved = [
        send(mine.at[:, (place + d) % share], piece_in.at[low, :, slot], a_send.at[d],
             a_recv.at[d], chips[d - 1])
        for d in range(1, share)
    ]
    piece_in[low, :, pl.ds(slot, 1), :] = mine[:, pl.ds(place, 1), :]

    for i in range(3, len(sources)):
        loads[i].wait()
    wet = mask_v[...].astype(F32)
    row_msg[0, 0:2, :] = fields[0, 0:2, :]
    row_msg[1, 0:2, :] = fields[0, BAND - 2 : BAND, :]
    for slot, index in ((2, 1), (3, 2), (4, 4), (5, 5)):
        row_msg[0, slot : slot + 1, :] = fields[index, 0:1, :]
        row_msg[1, slot : slot + 1, :] = fields[index, BAND - 1 : BAND, :]
    row_msg[0, 6:7, :] = wet[0:1]
    row_msg[1, 6:7, :] = wet[BAND - 1 : BAND]
    for slot, index in ((0, 0), (1, 1), (2, 2), (3, 3), (4, 5)):
        col_msg[0, :, 2 * slot : 2 * slot + 2] = fields[index, :, 0:2]
        col_msg[1, :, 2 * slot : 2 * slot + 2] = fields[index, :, width - 2 : width]
    col_msg[0, :, 10:12] = wet[:, 0:2]
    col_msg[1, :, 10:12] = wet[:, width - 2 : width]
    rims = [
        send(row_msg.at[0], row_in.at[1], h_send.at[0], h_recv.at[0], above),
        send(row_msg.at[1], row_in.at[0], h_send.at[1], h_recv.at[1], below),
        send(col_msg.at[0], col_in.at[1], h_send.at[2], h_recv.at[2], left),
        send(col_msg.at[1], col_in.at[0], h_send.at[3], h_recv.at[3], right),
    ]

    row = (z * 8 + 2 * iota((4, 128), 0) + iota((4, 128), 1) // SLOT) * BAND - 8
    row = row + iota((4, 128), 1) % SLOT
    cosine, sine = circle(row.astype(F32) + 0.5, 2 * GRID_LAT)
    ladder = (lane + 1).astype(F32)
    ratio = jnp.where(
        (lane >= 1) & (ladder <= order), jnp.log((2.0 * ladder + 1.0) / (2.0 * ladder)), 0.0
    )
    norm = jnp.sum(ratio, axis=1, keepdims=True) + jnp.where(order > 0.0, math.log(3.0), 0.0)
    log_scale = 0.5 * norm + order * jnp.log(jnp.abs(sine))
    to_scalar.wait()

    def block(inject, i, carry):
        current, previous, scale = carry
        base = pl.multiple_of(i * 16, 16)
        line, first = i // 8, (i % 8) * 16
        root = jnp.exp(0.5 * scale)
        for t in range(16):
            rest = ladder_s[16 + line, first + t] * previous
            if inject:
                rest = rest - jnp.where(base + t == number, 1.0, 0.0)
            latest = (ladder_s[line, first + t] * cosine) * current - rest
            raw[4 * t : 4 * t + 4, :] = latest
            current, previous = latest, current
        for k in range(4):
            factor = root[k : k + 1]
            high, low = halves(raw[pl.ds(k, 16, stride=4), :] * factor * factor)
            table_h[pl.ds(base, 16), 128 * k : 128 * k + 128] = high
            table_l[pl.ds(base, 16), 128 * k : 128 * k + 128] = low
        large = jnp.maximum(jnp.abs(current), jnp.abs(previous)) > 2.0**20
        factor = jnp.where(large, 2.0**-40, 1.0)
        shift = jnp.where(large, 40.0 * math.log(2.0), 0.0)
        return current * factor, previous * factor, scale + shift

    zero = jnp.zeros((4, 128), F32)
    blocks = length // 16
    early = min(8, blocks)
    state = (zero, zero, log_scale)
    state = lax.fori_loop(0, early, functools.partial(block, True), state)
    lax.fori_loop(early, blocks, functools.partial(block, False), state)

    for copy in moved:
        copy.wait_recv()
    total = piece_in[0]
    for s in range(1, lows):
        total = total + piece_in[s]
    rows = jnp.concatenate([total[:, k] for k in range(8)], axis=1)
    high = rows.astype(BF16).astype(F32)
    rows = jnp.concatenate([high, rows - high], axis=0).astype(BF16)
    product = rows_dot_t(rows, table_h[...]) + rows_dot_t(rows, table_l[...])
    coef[...] = product[0:2] + product[2:4]
    gathered = [
        send(coef, coef_in.at[d], c_send.at[d], c_recv.at[d], z_peers[d - 1])
        for d in range(1, depths)
    ]

    for copy in rims:
        copy.wait_recv()
    sub_row = band * BAND - 8 + iota((SLOT, 128), 0)
    band_sine = circle(sub_row.astype(F32) + 0.5, 2 * GRID_LAT)[1]
    out_sine[...] = band_sine
    body = slice(8, 8 + BAND)
    for index in range(6):
        out_fields[index, body, 0:width] = fields[index]
    out_fields[6, body, 0:width] = wet
    out_fields[0, 6:8, 0:width] = row_in[0, 0:2, :]
    out_fields[0, 56:58, 0:width] = row_in[1, 0:2, :]
    for slot, index in ((2, 1), (3, 2), (4, 4), (5, 5), (6, 6)):
        out_fields[index, 7:8, 0:width] = row_in[0, slot : slot + 1, :]
        out_fields[index, 56:57, 0:width] = row_in[1, slot : slot + 1, :]
    for slot, index in ((0, 0), (1, 1), (2, 2), (3, 3), (4, 5), (5, 6)):
        out_fields[index, body, wide - 2 : wide] = col_in[0, :, 2 * slot : 2 * slot + 2]
        out_fields[index, body, width : width + 2] = col_in[1, :, 2 * slot : 2 * slot + 2]
    meridional = 0.1 * GRID_LAT / GRID_LON

    def prepare(r, carry):
        at = pl.ds(pl.multiple_of(8 * r, 8), 8)
        u = out_fields[1, at, :]
        v = out_fields[2, at, :]
        inverse = 1.0 / out_fields[5, at, :]
        damping = 1.0 + FRICTION * jnp.sqrt(u * u + v * v) * inverse
        share = out_fields[6, at, :] / damping
        zonal_step = STEP_RATIO / out_sine[at, 0:1]
        out_fields[1, at, :] = share * (u + out_fields[3, at, :] * inverse)
        out_fields[2, at, :] = share * zonal_step
        out_fields[3, at, :] = share * (v + out_fields[4, at, :] * inverse)
        out_fields[4, at, :] = share * meridional
        return carry

    lax.fori_loop(0, SLOT // 8, prepare, 0)

    for copy in gathered:
        copy.wait_recv()
    whole = coef[...]
    for d in range(1, depths):
        whole = whole + coef_in[d]
    degrees = love_v.shape[0]
    weight = love_v[...].reshape(1, degrees) / (2.0 * iota((1, degrees), 1).astype(F32) + 1.0)
    weight = jnp.concatenate([weight, jnp.zeros((1, length - degrees), F32)], axis=1)
    whole = whole * weight
    high = whole.astype(BF16).astype(F32)
    whole = jnp.concatenate([high, whole - high], axis=0).astype(BF16)
    product = rows_dot(whole, table_h[...]) + rows_dot(whole, table_l[...])
    product = product[0:2] + product[2:4]
    for k in range(4):
        back_out[k] = product[:, 128 * k : 128 * k + 128]
    returned = [
        send(back_out.at[(x + d) % 4], spec_in.at[core, :, place], s_send.at[d], s_recv.at[d],
             chips[d - 1])
        for d in range(1, share)
    ]
    spec_in[core, :, pl.ds(place, 1), :] = back_out[x].reshape(2, 1, 128)
    for copy in returned:
        copy.wait_recv()
    last = send(spec_in.at[core], spec_in.at[core], last_send.at[0], last_recv.at[0], partner)
    for copy in sends[:-1]:
        copy.wait_send()
    out_spec[pl.ds(core, 1)] = spec_in[pl.ds(core, 1)].reshape(1, 2 * share, 128)
    last.wait_recv()
    out_spec[pl.ds(1 - core, 1)] = spec_in[pl.ds(1 - core, 1)].reshape(1, 2 * share, 128)
    last.wait_send()


def update_kernel(
    bands, width, wide,
    spec, th, tl, fields, sine,
    new_elevation, new_velocity, loading,
    surface, south_flux, loads,
):
    band = lax.axis_index("lat")

    source = iota((SLOT, 128), 0) + SLOT * (band % 2)
    move = jnp.where(iota((SLOT, 128), 1) == source, 1.0, 0.0).astype(BF16)
    high, low = halves(spec[...].reshape(th.shape[0], 128))
    high = rows_dot_t(move, high).astype(BF16)
    low = rows_dot_t(move, low).astype(BF16)
    t_high = th[...]
    loads[...] = rows_dot(high, t_high) + rows_dot(low, t_high) + rows_dot(high, tl[...])

    meridional = 0.1 * GRID_LAT / GRID_LON
    sub = iota((8, 1), 0)
    for r in range(8):
        at = slice(8 * r, 8 * r + 8)
        row = band * BAND - 8 + 8 * r + sub
        inside = (row >= 0) & (row < GRID_LAT)
        load = loads[at, :]
        surface[8 + 8 * r : 16 + 8 * r, :] = jnp.where(inside, fields[0, at, :] - load, 0.0)
        if 1 <= r <= 6:
            loading[0, 8 * r - 8 : 8 * r, :] = load[:, 0:width]
    for r in range(8):
        at = slice(8 * r, 8 * r + 8)
        row = band * BAND - 8 + 8 * r + sub
        inside = (row >= 0) & (row < GRID_LAT)
        change = surface[9 + 8 * r : 17 + 8 * r, :] - surface[7 + 8 * r : 15 + 8 * r, :]
        new_v = fields[3, at, :] - fields[4, at, :] * change
        flux = sine[at, 0:1] * fields[5, at, :] * new_v
        south_flux[at, :] = jnp.where(inside, flux, 0.0)
        if 1 <= r <= 6:
            new_velocity[0, 1, 8 * r - 8 : 8 * r, :] = new_v[:, 0:width]
    for r in range(1, 7):
        at = slice(8 * r, 8 * r + 8)
        here = surface[8 + 8 * r : 16 + 8 * r, :]
        change = pltpu.roll(here, wide - 1, 1) - pltpu.roll(here, 1, 1)
        new_u = fields[1, at, :] - fields[2, at, :] * change
        flux = fields[5, at, :] * new_u
        east = pltpu.roll(flux, wide - 1, 1) - pltpu.roll(flux, 1, 1)
        down = south_flux[8 * r + 1 : 8 * r + 9, :] - south_flux[8 * r - 1 : 8 * r + 7, :]
        row_sine = sine[at, 0:1]
        tendency = (STEP_RATIO / row_sine) * east + (meridional / row_sine) * down
        level = fields[0, at, :] - fields[6, at, :] * tendency
        new_velocity[0, 0, 8 * r - 8 : 8 * r, :] = new_u[:, 0:width]
        new_elevation[0, 8 * r - 8 : 8 * r, :] = level[:, 0:width]


def local(bands, sectors, elevation, velocity, wind_forcing, ocean_depth, wet_mask, love_factor,
          wavenumbers):
    width = elevation.shape[2]
    wide = -(-(width + 18) // 128) * 128
    length = -(-DEGREES // 16) * 16
    depths = bands // PILE
    share = 4 * sectors
    vmem = pl.BlockSpec(memory_space=pltpu.VMEM)
    hbm = pl.BlockSpec(memory_space=HBM)
    dma = pltpu.SemaphoreType.DMA
    shared = pl.pallas_call(
        functools.partial(spectral_kernel, bands, sectors, width, wide, length),
        out_shape=[
            jax.ShapeDtypeStruct((2, 2 * share, 128), F32),
            jax.ShapeDtypeStruct((4 * share, wide), BF16),
            jax.ShapeDtypeStruct((4 * share, wide), BF16),
            jax.ShapeDtypeStruct((7, SLOT, wide), F32),
            jax.ShapeDtypeStruct((SLOT, 128), F32),
        ],
        in_specs=[hbm] * 7,
        out_specs=[vmem] * 5,
        scratch_shapes=[
            pltpu.SMEM((8 * sectors,), jnp.int32),
            pltpu.VMEM((6, BAND, width), F32),
            pltpu.VMEM((BAND, width), jnp.int32),
            pltpu.VMEM((DEGREES,), F32),
            pltpu.VMEM((SLOT, wide), F32),
            pltpu.VMEM((2, 2 * share, SLOT), F32),
            pltpu.VMEM((2 * share, SLOT), F32),
            pltpu.VMEM((2, share, SLOT), F32),
            pltpu.VMEM((sectors // 2, 2, 8, SLOT), F32),
            pltpu.VMEM((2, length), F32),
            pltpu.VMEM((depths, 2, length), F32),
            pltpu.VMEM((4, 2, 128), F32),
            pltpu.VMEM((2, 8, width), F32),
            pltpu.VMEM((2, 8, width), F32),
            pltpu.VMEM((2, BAND, 128), F32),
            pltpu.VMEM((2, BAND, 128), F32),
            pltpu.VMEM((32, 128), F32),
            pltpu.SMEM((32, 128), F32),
            pltpu.VMEM((64, 128), F32),
            pltpu.VMEM((length, 512), BF16),
            pltpu.VMEM((length, 512), BF16),
            pltpu.VMEM((2, 2, share, 128), F32),
            dma((10,)),
            dma((1,)), dma((1,)),
            dma((share,)), dma((share,)),
            dma((depths,)), dma((depths,)),
            dma((share,)), dma((share,)),
            dma((1,)), dma((1,)),
            dma((4,)), dma((4,)),
        ],
        compiler_params=pltpu.CompilerParams(
            collective_id=0, has_side_effects=True, vmem_limit_bytes=24 * 1024 * 1024
        ),
        name="spectral",
    )(*[
        pltpu.with_memory_space_constraint(array, HBM)
        for array in (elevation, velocity, wind_forcing, ocean_depth, wet_mask,
                      love_factor, wavenumbers)
    ])
    return pl.pallas_call(
        functools.partial(update_kernel, bands, width, wide),
        out_shape=[
            jax.ShapeDtypeStruct(elevation.shape, F32),
            jax.ShapeDtypeStruct(velocity.shape, F32),
            jax.ShapeDtypeStruct(elevation.shape, F32),
        ],
        in_specs=[vmem] * 5,
        out_specs=[vmem] * 3,
        scratch_shapes=[
            pltpu.VMEM((SLOT + 16, wide), F32),
            pltpu.VMEM((SLOT, wide), F32),
            pltpu.VMEM((SLOT, wide), F32),
        ],
        compiler_params=pltpu.CompilerParams(vmem_limit_bytes=24 * 1024 * 1024),
        name="update",
    )(*shared)


def solution(mesh):
    bands, sectors = mesh.shape["lat"], mesh.shape["lon"]
    return jax.shard_map(
        functools.partial(local, bands, sectors),
        mesh=mesh,
        in_specs=(
            P(None, "lat", "lon"),
            P(None, None, "lat", "lon"),
            P(None, "lat", "lon"),
            P("lat", "lon"),
            P("lat", "lon"),
            P(),
            P(),
        ),
        out_specs=(P(None, "lat", "lon"), P(None, None, "lat", "lon"), P(None, "lat", "lon")),
        check_vma=False,
    )
```

```python
import functools
import math

import jax
import jax.numpy as jnp
from jax import lax
from jax.experimental import pallas as pl
from jax.experimental.pallas import tpu as pltpu
from jax.sharding import PartitionSpec as P

GRID_LAT = 3072
GRID_LON = 8640
DEGREES = 1081
STEP_RATIO = 0.05
FRICTION = 0.1

BAND = 48
SLOT = 64
PILE = 8
F32 = jnp.float32
BF16 = jnp.bfloat16
MESH = pl.DeviceIdType.MESH
HBM = pltpu.MemorySpace.HBM


def iota(shape, dim):
    return lax.broadcasted_iota(jnp.int32, shape, dim)


def halves(x):
    high = x.astype(BF16)
    return high, (x - high.astype(F32)).astype(BF16)


def rows_dot(a, b):
    return lax.dot_general(a, b, (((1,), (0,)), ((), ())), preferred_element_type=F32)


def rows_dot_t(a, b):
    return lax.dot_general(a, b, (((1,), (1,)), ((), ())), preferred_element_type=F32)


def circle(phase, period):
    turns = jnp.floor(phase * (4.0 / period) + 0.5)
    t = (phase - turns * (period / 4.0)) * (2.0 * math.pi / period)
    t2 = t * t
    s = t * (1.0 + t2 * (-1.0 / 6 + t2 * (1.0 / 120 + t2 * (-1.0 / 5040 + t2 * (1.0 / 362880)))))
    c = 1.0 + t2 * (-0.5 + t2 * (1.0 / 24 + t2 * (-1.0 / 720 + t2 * (1.0 / 40320))))
    quarter = turns.astype(jnp.int32) & 3
    odd = (quarter & 1) == 1
    cosine = jnp.where(odd, s, c)
    sine = jnp.where(odd, c, s)
    cosine = jnp.where((quarter == 1) | (quarter == 2), -cosine, cosine)
    sine = jnp.where(quarter >= 2, -sine, sine)
    return cosine, sine


def spectral_kernel(
    bands, sectors, width, wide, length,
    elevation, velocity, wind, depth, mask, love, waves_hbm,
    out_spec, out_th, out_tl, out_fields, out_sine,
    numbers, fields, mask_v, love_v, x_pad, part, pair_in, mine, piece_in, coef, coef_in,
    back_out, row_msg, row_in, col_msg, col_in,
    ladder_v, ladder_s, raw, table_h, table_l, spec_in,
    load_sem, pair_send, pair_recv, a_send, a_recv, c_send, c_recv,
    s_send, s_recv, last_send, last_recv, h_send, h_recv,
):
    depths = bands // PILE
    lows = sectors // 2
    share = 4 * sectors
    band = lax.axis_index("lat")
    sector = lax.axis_index("lon")
    z, x, half = band // 8, (band // 2) % 4, band % 2
    low, core = sector // 2, sector % 2

    sources = [
        (waves_hbm, numbers), (mask, mask_v), (elevation.at[0], fields.at[0]), (love, love_v),
        (velocity.at[0, 0], fields.at[1]), (velocity.at[0, 1], fields.at[2]),
        (wind.at[0], fields.at[3]), (wind.at[1], fields.at[4]), (depth, fields.at[5]),
    ]
    loads = [pltpu.make_async_copy(a, b, load_sem.at[i]) for i, (a, b) in enumerate(sources)]
    for copy in loads:
        copy.start()

    above = ((band + bands - 1) % bands, sector)
    below = ((band + 1) % bands, sector)
    left = (band, (sector + sectors - 1) % sectors)
    right = (band, (sector + 1) % sectors)

    y = half * lows + low
    place = y * 4 + x

    def chip(t):
        return (z * 8 + (t % 4) * 2 + t // 4 // lows, (t // 4 % lows) * 2 + core)

    steps = sorted(
        ((dy, dx) for dy in range(sectors) for dx in range(4) if dy or dx),
        key=lambda s: -min(s[0], sectors - s[0]) - min(s[1], 4 - s[1]),
    )
    places = [((y + dy) % sectors) * 4 + (x + dx) % 4 for dy, dx in steps]
    z_steps = sorted(range(1, depths), key=lambda d: -min(d, depths - d))

    partner = (band, low * 2 + 1 - core)
    chips = [chip(t) for t in places]
    z_peers = [(((z + d) % depths) * 8 + x * 2 + half, sector) for d in z_steps]
    peers = chips[:8] + z_peers + chips[8:] + [above, below, left, right, partner]
    barrier = pltpu.get_barrier_semaphore()
    for peer in peers:
        pl.semaphore_signal(barrier, inc=1, device_id=peer, device_id_type=MESH)

    loads[0].wait()

    lane = iota((1, 128), 1)
    sub = iota((16, 128), 0)

    def zonal(s, carry):
        waves = jnp.zeros((16, 128), F32)
        for p in range(16):
            waves = jnp.where(sub == p, numbers[s * 16 + p].astype(F32), waves)
        at = pl.multiple_of((s // (share // 16)) * 2 * share + (s % (share // 16)) * 16, 16)
        for tile in range(wide // 128):
            t = lane + tile * 128
            column = sector * width + jnp.where(t < width + 16, t, t - wide)
            cosine, sine = circle(waves * column.astype(F32), GRID_LON)
            high, low_part = halves(cosine)
            out_th[pl.ds(at, 16), tile * 128 : tile * 128 + 128] = high
            out_tl[pl.ds(at, 16), tile * 128 : tile * 128 + 128] = low_part
            high, low_part = halves(sine)
            out_th[pl.ds(at + share, 16), tile * 128 : tile * 128 + 128] = high
            out_tl[pl.ds(at + share, 16), tile * 128 : tile * 128 + 128] = low_part
        return carry

    lax.fori_loop(0, share // 8, zonal, 0)

    x_pad[...] = jnp.zeros_like(x_pad)
    loads[1].wait()
    loads[2].wait()
    x_pad[8:56, 0:width] = fields[0] * mask_v[...].astype(F32)
    x_high, x_low = halves(x_pad[...])
    t_high = out_th[...]
    sums = (
        rows_dot_t(t_high, x_high) + rows_dot_t(t_high, x_low) + rows_dot_t(out_tl[...], x_high)
    )
    part[0] = sums[0 : 2 * share]
    part[1] = sums[2 * share : 4 * share]

    pl.semaphore_wait(barrier, len(peers))
    sends = []

    def send(src, dst, send_sem, recv_sem, peer):
        copy = pltpu.make_async_remote_copy(
            src_ref=src, dst_ref=dst, send_sem=send_sem, recv_sem=recv_sem,
            device_id=peer, device_id_type=MESH,
        )
        copy.start()
        sends.append(copy)
        return copy

    pair = send(part.at[1 - core], pair_in, pair_send.at[0], pair_recv.at[0], partner)

    number = numbers[core * share + place]
    order = number.astype(F32)
    degree = (iota((16, 128), 0) * 128 + iota((16, 128), 1)).astype(F32)
    active = degree > order
    gap = jnp.where(active, degree * degree - order * order, 1.0)
    raising = jnp.sqrt((4.0 * degree * degree - 1.0) / gap)
    lower = degree - 1.0
    under = jnp.where(active, lower * lower - order * order, 0.0)
    over = jnp.where(active, 4.0 * lower * lower - 1.0, 1.0)
    raising = jnp.where(active, raising, 0.0)
    ladder_v[0:16, :] = raising
    ladder_v[16:32, :] = raising * jnp.sqrt(under / over)
    to_scalar = pltpu.make_async_copy(ladder_v, ladder_s, load_sem.at[len(sources)])
    to_scalar.start()

    slot_row = band * BAND - 8 + iota((1, SLOT), 1)
    slot_sine = circle(slot_row.astype(F32) + 0.5, 2 * GRID_LAT)[1]
    weights = slot_sine * (math.pi / (2.0 * GRID_LAT) / GRID_LON)
    own = part[core]
    pair.wait_recv()
    total = (own + pair_in[...]) * weights
    mine[0] = total[0:share]
    mine[1] = total[share : 2 * share]
    slot = 2 * x + half
    moved = [
        send(mine.at[:, t], piece_in.at[low, :, slot], a_send.at[n], a_recv.at[n], chips[n])
        for n, t in enumerate(places)
    ]
    piece_in[low, :, pl.ds(slot, 1), :] = mine[:, pl.ds(place, 1), :]

    for i in range(3, len(sources)):
        loads[i].wait()
    wet = mask_v[...].astype(F32)
    row_msg[0, 0:2, :] = fields[0, 0:2, :]
    row_msg[1, 0:2, :] = fields[0, BAND - 2 : BAND, :]
    for slot, index in ((2, 1), (3, 2), (4, 4), (5, 5)):
        row_msg[0, slot : slot + 1, :] = fields[index, 0:1, :]
        row_msg[1, slot : slot + 1, :] = fields[index, BAND - 1 : BAND, :]
    row_msg[0, 6:7, :] = wet[0:1]
    row_msg[1, 6:7, :] = wet[BAND - 1 : BAND]
    for slot, index in ((0, 0), (1, 1), (2, 2), (3, 3), (4, 5)):
        col_msg[0, :, 2 * slot : 2 * slot + 2] = fields[index, :, 0:2]
        col_msg[1, :, 2 * slot : 2 * slot + 2] = fields[index, :, width - 2 : width]
    col_msg[0, :, 10:12] = wet[:, 0:2]
    col_msg[1, :, 10:12] = wet[:, width - 2 : width]
    rims = [
        send(row_msg.at[0], row_in.at[1], h_send.at[0], h_recv.at[0], above),
        send(row_msg.at[1], row_in.at[0], h_send.at[1], h_recv.at[1], below),
        send(col_msg.at[0], col_in.at[1], h_send.at[2], h_recv.at[2], left),
        send(col_msg.at[1], col_in.at[0], h_send.at[3], h_recv.at[3], right),
    ]

    row = (z * 8 + 2 * iota((4, 128), 0) + iota((4, 128), 1) // SLOT) * BAND - 8
    row = row + iota((4, 128), 1) % SLOT
    cosine, sine = circle(row.astype(F32) + 0.5, 2 * GRID_LAT)
    ladder = (lane + 1).astype(F32)
    ratio = jnp.where(
        (lane >= 1) & (ladder <= order), jnp.log((2.0 * ladder + 1.0) / (2.0 * ladder)), 0.0
    )
    norm = jnp.sum(ratio, axis=1, keepdims=True) + jnp.where(order > 0.0, math.log(3.0), 0.0)
    log_scale = 0.5 * norm + order * jnp.log(jnp.abs(sine))
    to_scalar.wait()

    def block(inject, i, carry):
        current, previous, scale = carry
        base = pl.multiple_of(i * 16, 16)
        line, first = i // 8, (i % 8) * 16
        root = jnp.exp(0.5 * scale)
        for t in range(16):
            rest = ladder_s[16 + line, first + t] * previous
            if inject:
                rest = rest - jnp.where(base + t == number, 1.0, 0.0)
            latest = (ladder_s[line, first + t] * cosine) * current - rest
            raw[4 * t : 4 * t + 4, :] = latest
            current, previous = latest, current
        for k in range(4):
            factor = root[k : k + 1]
            high, low = halves(raw[pl.ds(k, 16, stride=4), :] * factor * factor)
            table_h[pl.ds(base, 16), 128 * k : 128 * k + 128] = high
            table_l[pl.ds(base, 16), 128 * k : 128 * k + 128] = low
        large = jnp.maximum(jnp.abs(current), jnp.abs(previous)) > 2.0**20
        factor = jnp.where(large, 2.0**-40, 1.0)
        shift = jnp.where(large, 40.0 * math.log(2.0), 0.0)
        return current * factor, previous * factor, scale + shift

    zero = jnp.zeros((4, 128), F32)
    blocks = length // 16
    early = min(8, blocks)
    state = (zero, zero, log_scale)
    state = lax.fori_loop(0, early, functools.partial(block, True), state)
    lax.fori_loop(early, blocks, functools.partial(block, False), state)

    for copy in moved:
        copy.wait_recv()
    total = piece_in[0]
    for s in range(1, lows):
        total = total + piece_in[s]
    rows = jnp.concatenate([total[:, k] for k in range(8)], axis=1)
    high = rows.astype(BF16).astype(F32)
    rows = jnp.concatenate([high, rows - high], axis=0).astype(BF16)
    cut = min(512, length // 2 // 128 * 128)
    parts = [slice(0, cut), slice(cut, length)] if cut else [slice(0, length)]
    gathered = []
    for h, part_rows in enumerate(parts):
        product = rows_dot_t(rows, table_h[part_rows, :]) + rows_dot_t(rows, table_l[part_rows, :])
        coef[:, part_rows] = product[0:2] + product[2:4]
        gathered.append([
            send(coef.at[:, part_rows], coef_in.at[d, :, part_rows], c_send.at[h, d],
                 c_recv.at[h, d], peer)
            for d, peer in zip(z_steps, z_peers)
        ])

    for copy in rims:
        copy.wait_recv()
    sub_row = band * BAND - 8 + iota((SLOT, 128), 0)
    band_sine = circle(sub_row.astype(F32) + 0.5, 2 * GRID_LAT)[1]
    out_sine[...] = band_sine
    body = slice(8, 8 + BAND)
    for index in range(6):
        out_fields[index, body, 0:width] = fields[index]
    out_fields[6, body, 0:width] = wet
    out_fields[0, 6:8, 0:width] = row_in[0, 0:2, :]
    out_fields[0, 56:58, 0:width] = row_in[1, 0:2, :]
    for slot, index in ((2, 1), (3, 2), (4, 4), (5, 5), (6, 6)):
        out_fields[index, 7:8, 0:width] = row_in[0, slot : slot + 1, :]
        out_fields[index, 56:57, 0:width] = row_in[1, slot : slot + 1, :]
    for slot, index in ((0, 0), (1, 1), (2, 2), (3, 3), (4, 5), (5, 6)):
        out_fields[index, body, wide - 2 : wide] = col_in[0, :, 2 * slot : 2 * slot + 2]
        out_fields[index, body, width : width + 2] = col_in[1, :, 2 * slot : 2 * slot + 2]
    meridional = 0.1 * GRID_LAT / GRID_LON

    def prepare(r, carry):
        at = pl.ds(pl.multiple_of(8 * r, 8), 8)
        u = out_fields[1, at, :]
        v = out_fields[2, at, :]
        inverse = 1.0 / out_fields[5, at, :]
        damping = 1.0 + FRICTION * jnp.sqrt(u * u + v * v) * inverse
        share = out_fields[6, at, :] / damping
        zonal_step = STEP_RATIO / out_sine[at, 0:1]
        out_fields[1, at, :] = share * (u + out_fields[3, at, :] * inverse)
        out_fields[2, at, :] = share * zonal_step
        out_fields[3, at, :] = share * (v + out_fields[4, at, :] * inverse)
        out_fields[4, at, :] = share * meridional
        return carry

    lax.fori_loop(0, SLOT // 8, prepare, 0)

    degrees = love_v.shape[0]
    weight = love_v[...].reshape(1, degrees) / (2.0 * iota((1, degrees), 1).astype(F32) + 1.0)
    weight = jnp.concatenate([weight, jnp.zeros((1, length - degrees), F32)], axis=1)
    product = 0.0
    for part_rows, copies in zip(parts, gathered):
        for copy in copies:
            copy.wait_recv()
        whole = coef[:, part_rows]
        for d in range(1, depths):
            whole = whole + coef_in[d, :, part_rows]
        whole = whole * weight[:, part_rows]
        high = whole.astype(BF16).astype(F32)
        whole = jnp.concatenate([high, whole - high], axis=0).astype(BF16)
        product = product + rows_dot(whole, table_h[part_rows, :])
        product = product + rows_dot(whole, table_l[part_rows, :])
    product = product[0:2] + product[2:4]
    for k in range(4):
        back_out[k] = product[:, 128 * k : 128 * k + 128]
    returned = [
        send(back_out.at[t % 4], spec_in.at[core, :, place], s_send.at[n], s_recv.at[n],
             chips[n])
        for n, t in enumerate(places)
    ]
    spec_in[core, :, pl.ds(place, 1), :] = back_out[x].reshape(2, 1, 128)
    for copy in returned:
        copy.wait_recv()
    last = send(spec_in.at[core], spec_in.at[core], last_send.at[0], last_recv.at[0], partner)
    for copy in sends[:-1]:
        copy.wait_send()
    out_spec[pl.ds(core, 1)] = spec_in[pl.ds(core, 1)].reshape(1, 2 * share, 128)
    last.wait_recv()
    out_spec[pl.ds(1 - core, 1)] = spec_in[pl.ds(1 - core, 1)].reshape(1, 2 * share, 128)
    last.wait_send()


def update_kernel(
    bands, width, wide,
    spec, th, tl, fields, sine,
    new_elevation, new_velocity, loading,
    surface, south_flux, loads, results, out_sem,
):
    band = lax.axis_index("lat")
    copies = []

    def store(index, target, rows):
        copy = pltpu.make_async_copy(
            results.at[index, rows], target.at[rows], out_sem.at[len(copies)]
        )
        copy.start()
        copies.append(copy)

    source = iota((SLOT, 128), 0) + SLOT * (band % 2)
    move = jnp.where(iota((SLOT, 128), 1) == source, 1.0, 0.0).astype(BF16)
    high, low = halves(spec[...].reshape(th.shape[0], 128))
    high = rows_dot_t(move, high).astype(BF16)
    low = rows_dot_t(move, low).astype(BF16)
    t_high = th[...]
    loads[...] = rows_dot(high, t_high) + rows_dot(low, t_high) + rows_dot(high, tl[...])

    meridional = 0.1 * GRID_LAT / GRID_LON
    sub = iota((8, 1), 0)
    for r in range(8):
        at = slice(8 * r, 8 * r + 8)
        row = band * BAND - 8 + 8 * r + sub
        inside = (row >= 0) & (row < GRID_LAT)
        load = loads[at, :]
        surface[8 + 8 * r : 16 + 8 * r, :] = jnp.where(inside, fields[0, at, :] - load, 0.0)
        if 1 <= r <= 6:
            results[0, 8 * r - 8 : 8 * r, :] = load[:, 0:width]
    store(0, loading.at[0], pl.ds(0, BAND))
    for r in range(8):
        at = slice(8 * r, 8 * r + 8)
        row = band * BAND - 8 + 8 * r + sub
        inside = (row >= 0) & (row < GRID_LAT)
        change = surface[9 + 8 * r : 17 + 8 * r, :] - surface[7 + 8 * r : 15 + 8 * r, :]
        new_v = fields[3, at, :] - fields[4, at, :] * change
        flux = sine[at, 0:1] * fields[5, at, :] * new_v
        south_flux[at, :] = jnp.where(inside, flux, 0.0)
        if 1 <= r <= 6:
            results[1, 8 * r - 8 : 8 * r, :] = new_v[:, 0:width]
    store(1, new_velocity.at[0, 1], pl.ds(0, BAND))
    for r in range(1, 7):
        at = slice(8 * r, 8 * r + 8)
        here = surface[8 + 8 * r : 16 + 8 * r, :]
        change = pltpu.roll(here, wide - 1, 1) - pltpu.roll(here, 1, 1)
        new_u = fields[1, at, :] - fields[2, at, :] * change
        flux = fields[5, at, :] * new_u
        east = pltpu.roll(flux, wide - 1, 1) - pltpu.roll(flux, 1, 1)
        down = south_flux[8 * r + 1 : 8 * r + 9, :] - south_flux[8 * r - 1 : 8 * r + 7, :]
        row_sine = sine[at, 0:1]
        tendency = (STEP_RATIO / row_sine) * east + (meridional / row_sine) * down
        level = fields[0, at, :] - fields[6, at, :] * tendency
        results[2, 8 * r - 8 : 8 * r, :] = new_u[:, 0:width]
        results[3, 8 * r - 8 : 8 * r, :] = level[:, 0:width]
        if r % 2 == 0:
            store(2, new_velocity.at[0, 0], pl.ds(8 * r - 16, 16))
            store(3, new_elevation.at[0], pl.ds(8 * r - 16, 16))
    for copy in copies:
        copy.wait()


def local(bands, sectors, elevation, velocity, wind_forcing, ocean_depth, wet_mask, love_factor,
          wavenumbers):
    width = elevation.shape[2]
    wide = -(-(width + 18) // 128) * 128
    length = -(-DEGREES // 16) * 16
    depths = bands // PILE
    share = 4 * sectors
    vmem = pl.BlockSpec(memory_space=pltpu.VMEM)
    hbm = pl.BlockSpec(memory_space=HBM)
    dma = pltpu.SemaphoreType.DMA
    shared = pl.pallas_call(
        functools.partial(spectral_kernel, bands, sectors, width, wide, length),
        out_shape=[
            jax.ShapeDtypeStruct((2, 2 * share, 128), F32),
            jax.ShapeDtypeStruct((4 * share, wide), BF16),
            jax.ShapeDtypeStruct((4 * share, wide), BF16),
            jax.ShapeDtypeStruct((7, SLOT, wide), F32),
            jax.ShapeDtypeStruct((SLOT, 128), F32),
        ],
        in_specs=[hbm] * 7,
        out_specs=[vmem] * 5,
        scratch_shapes=[
            pltpu.SMEM((8 * sectors,), jnp.int32),
            pltpu.VMEM((6, BAND, width), F32),
            pltpu.VMEM((BAND, width), jnp.int32),
            pltpu.VMEM((DEGREES,), F32),
            pltpu.VMEM((SLOT, wide), F32),
            pltpu.VMEM((2, 2 * share, SLOT), F32),
            pltpu.VMEM((2 * share, SLOT), F32),
            pltpu.VMEM((2, share, SLOT), F32),
            pltpu.VMEM((sectors // 2, 2, 8, SLOT), F32),
            pltpu.VMEM((2, length), F32),
            pltpu.VMEM((depths, 2, length), F32),
            pltpu.VMEM((4, 2, 128), F32),
            pltpu.VMEM((2, 8, width), F32),
            pltpu.VMEM((2, 8, width), F32),
            pltpu.VMEM((2, BAND, 128), F32),
            pltpu.VMEM((2, BAND, 128), F32),
            pltpu.VMEM((32, 128), F32),
            pltpu.SMEM((32, 128), F32),
            pltpu.VMEM((64, 128), F32),
            pltpu.VMEM((length, 512), BF16),
            pltpu.VMEM((length, 512), BF16),
            pltpu.VMEM((2, 2, share, 128), F32),
            dma((10,)),
            dma((1,)), dma((1,)),
            dma((share,)), dma((share,)),
            dma((2, depths)), dma((2, depths)),
            dma((share,)), dma((share,)),
            dma((1,)), dma((1,)),
            dma((4,)), dma((4,)),
        ],
        compiler_params=pltpu.CompilerParams(
            collective_id=0, has_side_effects=True, vmem_limit_bytes=24 * 1024 * 1024
        ),
        name="spectral",
    )(*[
        pltpu.with_memory_space_constraint(array, HBM)
        for array in (elevation, velocity, wind_forcing, ocean_depth, wet_mask,
                      love_factor, wavenumbers)
    ])
    return pl.pallas_call(
        functools.partial(update_kernel, bands, width, wide),
        out_shape=[
            jax.ShapeDtypeStruct(elevation.shape, F32),
            jax.ShapeDtypeStruct(velocity.shape, F32),
            jax.ShapeDtypeStruct(elevation.shape, F32),
        ],
        in_specs=[vmem] * 5,
        out_specs=[hbm] * 3,
        scratch_shapes=[
            pltpu.VMEM((SLOT + 16, wide), F32),
            pltpu.VMEM((SLOT, wide), F32),
            pltpu.VMEM((SLOT, wide), F32),
            pltpu.VMEM((4, BAND, width), F32),
            dma((8,)),
        ],
        compiler_params=pltpu.CompilerParams(vmem_limit_bytes=24 * 1024 * 1024),
        name="update",
    )(*shared)


def solution(mesh):
    bands, sectors = mesh.shape["lat"], mesh.shape["lon"]
    return jax.shard_map(
        functools.partial(local, bands, sectors),
        mesh=mesh,
        in_specs=(
            P(None, "lat", "lon"),
            P(None, None, "lat", "lon"),
            P(None, "lat", "lon"),
            P("lat", "lon"),
            P("lat", "lon"),
            P(),
            P(),
        ),
        out_specs=(P(None, "lat", "lon"), P(None, None, "lat", "lon"), P(None, "lat", "lon")),
        check_vma=False,
    )
```

```python
import functools
import math

import jax
import jax.numpy as jnp
from jax import lax
from jax.experimental import pallas as pl
from jax.experimental.pallas import tpu as pltpu
from jax.sharding import PartitionSpec as P

GRID_LAT = 3072
GRID_LON = 8640
DEGREES = 1081
STEP_RATIO = 0.05
FRICTION = 0.1

BAND = 48
SLOT = 64
PILE = 8
F32 = jnp.float32
BF16 = jnp.bfloat16
MESH = pl.DeviceIdType.MESH
HBM = pltpu.MemorySpace.HBM
PRE = 8


def iota(shape, dim):
    return lax.broadcasted_iota(jnp.int32, shape, dim)


def halves(x):
    high = x.astype(BF16)
    return high, (x - high.astype(F32)).astype(BF16)


def rows_dot(a, b):
    return lax.dot_general(a, b, (((1,), (0,)), ((), ())), preferred_element_type=F32)


def rows_dot_t(a, b):
    return lax.dot_general(a, b, (((1,), (1,)), ((), ())), preferred_element_type=F32)


def circle(phase, period):
    turns = jnp.floor(phase * (4.0 / period) + 0.5)
    t = (phase - turns * (period / 4.0)) * (2.0 * math.pi / period)
    t2 = t * t
    s = t * (1.0 + t2 * (-1.0 / 6 + t2 * (1.0 / 120 + t2 * (-1.0 / 5040 + t2 * (1.0 / 362880)))))
    c = 1.0 + t2 * (-0.5 + t2 * (1.0 / 24 + t2 * (-1.0 / 720 + t2 * (1.0 / 40320))))
    quarter = turns.astype(jnp.int32) & 3
    odd = (quarter & 1) == 1
    cosine = jnp.where(odd, s, c)
    sine = jnp.where(odd, c, s)
    cosine = jnp.where((quarter == 1) | (quarter == 2), -cosine, cosine)
    sine = jnp.where(quarter >= 2, -sine, sine)
    return cosine, sine


def spectral_kernel(
    bands, sectors, width, wide, length,
    elevation, velocity, wind, depth, mask, love, waves_hbm,
    out_spec, out_th, out_tl, out_fields, out_sine,
    numbers, fields, mask_v, love_v, x_pad, part, piece_in, coef, coef_in,
    back_out, row_msg, row_in, col_msg, col_in,
    ladder_v, ladder_s, raw, table_h, table_l, spec_in,
    load_sem, a_send, a_recv, c_send, c_recv, s_send, s_recv, h_send, h_recv,
):
    depths = bands // PILE
    lows = sectors // 2
    share = 4 * sectors
    band = lax.axis_index("lat")
    sector = lax.axis_index("lon")
    z, x, half = band // 8, (band // 2) % 4, band % 2
    low, core = sector // 2, sector % 2

    sources = [
        (waves_hbm, numbers), (mask, mask_v), (elevation.at[0], fields.at[0]), (love, love_v),
        (velocity.at[0, 0], fields.at[1]), (velocity.at[0, 1], fields.at[2]),
        (wind.at[0], fields.at[3]), (wind.at[1], fields.at[4]), (depth, fields.at[5]),
    ]
    loads = [pltpu.make_async_copy(a, b, load_sem.at[i]) for i, (a, b) in enumerate(sources)]
    for copy in loads[:3]:
        copy.start()

    above = ((band + bands - 1) % bands, sector)
    below = ((band + 1) % bands, sector)
    left = (band, (sector + sectors - 1) % sectors)
    right = (band, (sector + 1) % sectors)

    y = half * lows + low
    place = y * 4 + x

    steps = sorted(
        ((dy, dx, dc) for dy in range(sectors) for dx in range(4) for dc in range(2)
         if dy or dx or dc),
        key=lambda s: -min(s[0], sectors - s[0]) - min(s[1], 4 - s[1]),
    )
    mates = []
    for dy, dx, dc in steps:
        peer_y, peer_x, peer_core = (y + dy) % sectors, (x + dx) % 4, (core + dc) % 2
        peer = (z * 8 + peer_x * 2 + peer_y // lows, (peer_y % lows) * 2 + peer_core)
        mates.append((peer, peer_core, peer_y * 4 + peer_x, peer_x))
    z_steps = sorted(range(1, depths), key=lambda d: -min(d, depths - d))

    plane = [mate[0] for mate in mates]
    z_peers = [(((z + d) % depths) * 8 + x * 2 + half, sector) for d in z_steps]
    peers = plane[:20] + z_peers + plane[20:] + [above, below, left, right]
    barrier = pltpu.get_barrier_semaphore()
    for peer in peers:
        pl.semaphore_signal(barrier, inc=1, device_id=peer, device_id_type=MESH)

    for copy in loads[3:]:
        copy.start()
    x_pad[...] = jnp.zeros_like(x_pad)
    loads[0].wait()

    lane = iota((1, 128), 1)
    sub = iota((16, 128), 0)

    def zonal(s, carry):
        waves = jnp.zeros((16, 128), F32)
        for p in range(16):
            waves = jnp.where(sub == p, numbers[s * 16 + p].astype(F32), waves)
        at = pl.multiple_of((s // (share // 16)) * 2 * share + (s % (share // 16)) * 16, 16)
        for tile in range(wide // 128):
            t = lane + tile * 128
            column = sector * width + jnp.where(t < width + 16, t, t - wide)
            cosine, sine = circle(waves * column.astype(F32), GRID_LON)
            high, low_part = halves(cosine)
            out_th[pl.ds(at, 16), tile * 128 : tile * 128 + 128] = high
            out_tl[pl.ds(at, 16), tile * 128 : tile * 128 + 128] = low_part
            high, low_part = halves(sine)
            out_th[pl.ds(at + share, 16), tile * 128 : tile * 128 + 128] = high
            out_tl[pl.ds(at + share, 16), tile * 128 : tile * 128 + 128] = low_part
        return carry

    lax.fori_loop(0, share // 8, zonal, 0)

    loads[1].wait()
    loads[2].wait()
    x_pad[8:56, 0:width] = fields[0] * mask_v[...].astype(F32)
    x_high, x_low = halves(x_pad[...])
    t_high = out_th[...]
    sums = (
        rows_dot_t(t_high, x_high) + rows_dot_t(t_high, x_low) + rows_dot_t(out_tl[...], x_high)
    )
    slot_row = band * BAND - 8 + iota((1, SLOT), 1)
    slot_sine = circle(slot_row.astype(F32) + 0.5, 2 * GRID_LAT)[1]
    sums = sums * (slot_sine * (math.pi / (2.0 * GRID_LAT) / GRID_LON))
    for c in range(2):
        for kind in range(2):
            at = (2 * c + kind) * share
            part[c, kind] = sums[at : at + share]

    pl.semaphore_wait(barrier, len(peers))
    sends = []

    def send(src, dst, send_sem, recv_sem, peer):
        copy = pltpu.make_async_remote_copy(
            src_ref=src, dst_ref=dst, send_sem=send_sem, recv_sem=recv_sem,
            device_id=peer, device_id_type=MESH,
        )
        copy.start()
        sends.append(copy)
        return copy

    slot = 2 * x + half
    moved = [
        send(part.at[c, :, t], piece_in.at[sector, :, slot], a_send.at[n], a_recv.at[n], peer)
        for n, (peer, c, t, _) in enumerate(mates)
    ]
    piece_in[sector, :, pl.ds(slot, 1), :] = part[core, :, pl.ds(place, 1), :]

    number = numbers[core * share + place]
    order = number.astype(F32)
    degree = (iota((16, 128), 0) * 128 + iota((16, 128), 1)).astype(F32)
    active = degree > order
    gap = jnp.where(active, degree * degree - order * order, 1.0)
    raising = jnp.sqrt((4.0 * degree * degree - 1.0) / gap)
    lower = degree - 1.0
    under = jnp.where(active, lower * lower - order * order, 0.0)
    over = jnp.where(active, 4.0 * lower * lower - 1.0, 1.0)
    raising = jnp.where(active, raising, 0.0)
    ladder_v[0:16, :] = raising
    ladder_v[16:32, :] = raising * jnp.sqrt(under / over)
    to_scalar = pltpu.make_async_copy(ladder_v, ladder_s, load_sem.at[len(sources)])
    to_scalar.start()

    for i in range(3, len(sources)):
        loads[i].wait()
    wet = mask_v[...].astype(F32)
    row_msg[0, 0:2, :] = fields[0, 0:2, :]
    row_msg[1, 0:2, :] = fields[0, BAND - 2 : BAND, :]
    for slot, index in ((2, 1), (3, 2), (4, 4), (5, 5)):
        row_msg[0, slot : slot + 1, :] = fields[index, 0:1, :]
        row_msg[1, slot : slot + 1, :] = fields[index, BAND - 1 : BAND, :]
    row_msg[0, 6:7, :] = wet[0:1]
    row_msg[1, 6:7, :] = wet[BAND - 1 : BAND]
    for slot, index in ((0, 0), (1, 1), (2, 2), (3, 3), (4, 5)):
        col_msg[0, :, 2 * slot : 2 * slot + 2] = fields[index, :, 0:2]
        col_msg[1, :, 2 * slot : 2 * slot + 2] = fields[index, :, width - 2 : width]
    col_msg[0, :, 10:12] = wet[:, 0:2]
    col_msg[1, :, 10:12] = wet[:, width - 2 : width]

    rims = [
        send(row_msg.at[0], row_in.at[1], h_send.at[0], h_recv.at[0], above),
        send(row_msg.at[1], row_in.at[0], h_send.at[1], h_recv.at[1], below),
        send(col_msg.at[0], col_in.at[1], h_send.at[2], h_recv.at[2], left),
        send(col_msg.at[1], col_in.at[0], h_send.at[3], h_recv.at[3], right),
    ]

    row = (z * 8 + 2 * iota((4, 128), 0) + iota((4, 128), 1) // SLOT) * BAND - 8
    row = row + iota((4, 128), 1) % SLOT
    cosine, sine = circle(row.astype(F32) + 0.5, 2 * GRID_LAT)
    ladder = (lane + 1).astype(F32)
    ratio = jnp.where(
        (lane >= 1) & (ladder <= order), jnp.log((2.0 * ladder + 1.0) / (2.0 * ladder)), 0.0
    )
    norm = jnp.sum(ratio, axis=1, keepdims=True) + jnp.where(order > 0.0, math.log(3.0), 0.0)
    log_scale = 0.5 * norm + order * jnp.log(jnp.abs(sine))
    to_scalar.wait()

    def block(inject, i, carry):
        current, previous, scale = carry
        base = pl.multiple_of(i * 16, 16)
        line, first = i // 8, (i % 8) * 16
        root = jnp.exp(0.5 * scale)
        for t in range(16):
            rest = ladder_s[16 + line, first + t] * previous
            if inject:
                rest = rest - jnp.where(base + t == number, 1.0, 0.0)
            latest = (ladder_s[line, first + t] * cosine) * current - rest
            raw[4 * t : 4 * t + 4, :] = latest
            current, previous = latest, current
        for k in range(4):
            factor = root[k : k + 1]
            high, low = halves(raw[pl.ds(k, 16, stride=4), :] * factor * factor)
            table_h[pl.ds(base, 16), 128 * k : 128 * k + 128] = high
            table_l[pl.ds(base, 16), 128 * k : 128 * k + 128] = low
        large = jnp.maximum(jnp.abs(current), jnp.abs(previous)) > 2.0**20
        factor = jnp.where(large, 2.0**-40, 1.0)
        shift = jnp.where(large, 40.0 * math.log(2.0), 0.0)
        return current * factor, previous * factor, scale + shift

    zero = jnp.zeros((4, 128), F32)
    blocks = length // 16
    early = min(8, blocks)
    state = (zero, zero, log_scale)
    state = lax.fori_loop(0, early, functools.partial(block, True), state)
    state = lax.fori_loop(early, min(PRE, blocks), functools.partial(block, False), state)

    lax.fori_loop(min(PRE, blocks), blocks, functools.partial(block, False), state)

    for copy in reversed(moved):
        copy.wait_recv()
    total = piece_in[0]
    for s in range(1, sectors):
        total = total + piece_in[s]
    rows = jnp.concatenate([total[:, k] for k in range(8)], axis=1)
    high = rows.astype(BF16).astype(F32)
    rows = jnp.concatenate([high, rows - high], axis=0).astype(BF16)
    cut = min(512, length // 2 // 128 * 128)
    parts = [slice(0, cut), slice(cut, length)] if cut else [slice(0, length)]
    gathered = []
    for h, part_rows in enumerate(parts):
        product = rows_dot_t(rows, table_h[part_rows, :]) + rows_dot_t(rows, table_l[part_rows, :])
        coef[:, part_rows] = product[0:2] + product[2:4]
        gathered.append([
            send(coef.at[:, part_rows], coef_in.at[d, :, part_rows], c_send.at[h, d],
                 c_recv.at[h, d], peer)
            for d, peer in zip(z_steps, z_peers)
        ])

    for copy in rims:
        copy.wait_recv()
    sub_row = band * BAND - 8 + iota((SLOT, 128), 0)
    band_sine = circle(sub_row.astype(F32) + 0.5, 2 * GRID_LAT)[1]
    out_sine[...] = band_sine
    body = slice(8, 8 + BAND)
    for index in range(6):
        out_fields[index, body, 0:width] = fields[index]
    out_fields[6, body, 0:width] = wet
    out_fields[0, 6:8, 0:width] = row_in[0, 0:2, :]
    out_fields[0, 56:58, 0:width] = row_in[1, 0:2, :]
    for slot, index in ((2, 1), (3, 2), (4, 4), (5, 5), (6, 6)):
        out_fields[index, 7:8, 0:width] = row_in[0, slot : slot + 1, :]
        out_fields[index, 56:57, 0:width] = row_in[1, slot : slot + 1, :]
    for slot, index in ((0, 0), (1, 1), (2, 2), (3, 3), (4, 5), (5, 6)):
        out_fields[index, body, wide - 2 : wide] = col_in[0, :, 2 * slot : 2 * slot + 2]
        out_fields[index, body, width : width + 2] = col_in[1, :, 2 * slot : 2 * slot + 2]
    meridional = 0.1 * GRID_LAT / GRID_LON

    def prepare(r, carry):
        at = pl.ds(pl.multiple_of(8 * r, 8), 8)
        u = out_fields[1, at, :]
        v = out_fields[2, at, :]
        inverse = 1.0 / out_fields[5, at, :]
        damping = 1.0 + FRICTION * jnp.sqrt(u * u + v * v) * inverse
        share = out_fields[6, at, :] / damping
        zonal_step = STEP_RATIO / out_sine[at, 0:1]
        out_fields[1, at, :] = share * (u + out_fields[3, at, :] * inverse)
        out_fields[2, at, :] = share * zonal_step
        out_fields[3, at, :] = share * (v + out_fields[4, at, :] * inverse)
        out_fields[4, at, :] = share * meridional
        return carry

    lax.fori_loop(0, SLOT // 8, prepare, 0)
    for copy in reversed(sends):
        copy.wait_send()
    sends.clear()

    degrees = love_v.shape[0]
    weight = love_v[...].reshape(1, degrees) / (2.0 * iota((1, degrees), 1).astype(F32) + 1.0)
    weight = jnp.concatenate([weight, jnp.zeros((1, length - degrees), F32)], axis=1)
    product = 0.0
    for part_rows, copies in zip(parts, gathered):
        for copy in reversed(copies):
            copy.wait_recv()
        whole = coef[:, part_rows]
        for d in range(1, depths):
            whole = whole + coef_in[d, :, part_rows]
        whole = whole * weight[:, part_rows]
        high = whole.astype(BF16).astype(F32)
        whole = jnp.concatenate([high, whole - high], axis=0).astype(BF16)
        product = product + rows_dot(whole, table_h[part_rows, :])
        product = product + rows_dot(whole, table_l[part_rows, :])
    product = product[0:2] + product[2:4]
    for k in range(4):
        back_out[k] = product[:, 128 * k : 128 * k + 128]
    returned = [
        send(back_out.at[k], spec_in.at[core, :, place], s_send.at[n], s_recv.at[n], peer)
        for n, (peer, _, _, k) in enumerate(mates)
    ]
    spec_in[core, :, pl.ds(place, 1), :] = back_out[x].reshape(2, 1, 128)
    for copy in reversed(sends):
        copy.wait_send()
    for copy in reversed(returned):
        copy.wait_recv()
    for c in range(2):
        out_spec[c] = spec_in[c].reshape(2 * share, 128)


def update_kernel(
    bands, width, wide,
    spec, th, tl, fields, sine,
    new_elevation, new_velocity, loading,
    surface, south_flux, loads, results, out_sem,
):
    band = lax.axis_index("lat")
    copies = []

    def store(index, target, rows):
        copy = pltpu.make_async_copy(
            results.at[index, rows], target.at[rows], out_sem.at[len(copies)]
        )
        copy.start()
        copies.append(copy)

    source = iota((SLOT, 128), 0) + SLOT * (band % 2)
    move = jnp.where(iota((SLOT, 128), 1) == source, 1.0, 0.0).astype(BF16)
    high, low = halves(spec[...].reshape(th.shape[0], 128))
    high = rows_dot_t(move, high).astype(BF16)
    low = rows_dot_t(move, low).astype(BF16)
    t_high = th[...]
    loads[...] = rows_dot(high, t_high) + rows_dot(low, t_high) + rows_dot(high, tl[...])

    meridional = 0.1 * GRID_LAT / GRID_LON
    sub = iota((8, 1), 0)
    for r in range(8):
        at = slice(8 * r, 8 * r + 8)
        row = band * BAND - 8 + 8 * r + sub
        inside = (row >= 0) & (row < GRID_LAT)
        load = loads[at, :]
        surface[8 + 8 * r : 16 + 8 * r, :] = jnp.where(inside, fields[0, at, :] - load, 0.0)
        if 1 <= r <= 6:
            results[0, 8 * r - 8 : 8 * r, :] = load[:, 0:width]
    store(0, loading.at[0], pl.ds(0, BAND))
    for r in range(8):
        at = slice(8 * r, 8 * r + 8)
        row = band * BAND - 8 + 8 * r + sub
        inside = (row >= 0) & (row < GRID_LAT)
        change = surface[9 + 8 * r : 17 + 8 * r, :] - surface[7 + 8 * r : 15 + 8 * r, :]
        new_v = fields[3, at, :] - fields[4, at, :] * change
        flux = sine[at, 0:1] * fields[5, at, :] * new_v
        south_flux[at, :] = jnp.where(inside, flux, 0.0)
        if 1 <= r <= 6:
            results[1, 8 * r - 8 : 8 * r, :] = new_v[:, 0:width]
    store(1, new_velocity.at[0, 1], pl.ds(0, BAND))
    for r in range(1, 7):
        at = slice(8 * r, 8 * r + 8)
        here = surface[8 + 8 * r : 16 + 8 * r, :]
        change = pltpu.roll(here, wide - 1, 1) - pltpu.roll(here, 1, 1)
        new_u = fields[1, at, :] - fields[2, at, :] * change
        flux = fields[5, at, :] * new_u
        east = pltpu.roll(flux, wide - 1, 1) - pltpu.roll(flux, 1, 1)
        down = south_flux[8 * r + 1 : 8 * r + 9, :] - south_flux[8 * r - 1 : 8 * r + 7, :]
        row_sine = sine[at, 0:1]
        tendency = (STEP_RATIO / row_sine) * east + (meridional / row_sine) * down
        level = fields[0, at, :] - fields[6, at, :] * tendency
        results[2, 8 * r - 8 : 8 * r, :] = new_u[:, 0:width]
        results[3, 8 * r - 8 : 8 * r, :] = level[:, 0:width]
        if r % 2 == 0:
            store(2, new_velocity.at[0, 0], pl.ds(8 * r - 16, 16))
            store(3, new_elevation.at[0], pl.ds(8 * r - 16, 16))
    for copy in copies:
        copy.wait()


def local(bands, sectors, elevation, velocity, wind_forcing, ocean_depth, wet_mask, love_factor,
          wavenumbers):
    width = elevation.shape[2]
    wide = -(-(width + 18) // 128) * 128
    length = -(-DEGREES // 16) * 16
    depths = bands // PILE
    share = 4 * sectors
    vmem = pl.BlockSpec(memory_space=pltpu.VMEM)
    hbm = pl.BlockSpec(memory_space=HBM)
    dma = pltpu.SemaphoreType.DMA
    shared = pl.pallas_call(
        functools.partial(spectral_kernel, bands, sectors, width, wide, length),
        out_shape=[
            jax.ShapeDtypeStruct((2, 2 * share, 128), F32),
            jax.ShapeDtypeStruct((4 * share, wide), BF16),
            jax.ShapeDtypeStruct((4 * share, wide), BF16),
            jax.ShapeDtypeStruct((7, SLOT, wide), F32),
            jax.ShapeDtypeStruct((SLOT, 128), F32),
        ],
        in_specs=[hbm] * 7,
        out_specs=[vmem] * 5,
        scratch_shapes=[
            pltpu.SMEM((8 * sectors,), jnp.int32),
            pltpu.VMEM((6, BAND, width), F32),
            pltpu.VMEM((BAND, width), jnp.int32),
            pltpu.VMEM((DEGREES,), F32),
            pltpu.VMEM((SLOT, wide), F32),
            pltpu.VMEM((2, 2, share, SLOT), F32),
            pltpu.VMEM((sectors, 2, 8, SLOT), F32),
            pltpu.VMEM((2, length), F32),
            pltpu.VMEM((depths, 2, length), F32),
            pltpu.VMEM((4, 2, 128), F32),
            pltpu.VMEM((2, 8, width), F32),
            pltpu.VMEM((2, 8, width), F32),
            pltpu.VMEM((2, BAND, 128), F32),
            pltpu.VMEM((2, BAND, 128), F32),
            pltpu.VMEM((32, 128), F32),
            pltpu.SMEM((32, 128), F32),
            pltpu.VMEM((64, 128), F32),
            pltpu.VMEM((length, 512), BF16),
            pltpu.VMEM((length, 512), BF16),
            pltpu.VMEM((2, 2, share, 128), F32),
            dma((10,)),
            dma((2 * share,)), dma((2 * share,)),
            dma((2, depths)), dma((2, depths)),
            dma((2 * share,)), dma((2 * share,)),
            dma((4,)), dma((4,)),
        ],
        compiler_params=pltpu.CompilerParams(
            collective_id=0, has_side_effects=True, vmem_limit_bytes=24 * 1024 * 1024
        ),
        name="spectral",
    )(*[
        pltpu.with_memory_space_constraint(array, HBM)
        for array in (elevation, velocity, wind_forcing, ocean_depth, wet_mask,
                      love_factor, wavenumbers)
    ])
    return pl.pallas_call(
        functools.partial(update_kernel, bands, width, wide),
        out_shape=[
            jax.ShapeDtypeStruct(elevation.shape, F32),
            jax.ShapeDtypeStruct(velocity.shape, F32),
            jax.ShapeDtypeStruct(elevation.shape, F32),
        ],
        in_specs=[vmem] * 5,
        out_specs=[hbm] * 3,
        scratch_shapes=[
            pltpu.VMEM((SLOT + 16, wide), F32),
            pltpu.VMEM((SLOT, wide), F32),
            pltpu.VMEM((SLOT, wide), F32),
            pltpu.VMEM((4, BAND, width), F32),
            dma((8,)),
        ],
        compiler_params=pltpu.CompilerParams(vmem_limit_bytes=24 * 1024 * 1024),
        name="update",
    )(*shared)


def solution(mesh):
    bands, sectors = mesh.shape["lat"], mesh.shape["lon"]
    return jax.shard_map(
        functools.partial(local, bands, sectors),
        mesh=mesh,
        in_specs=(
            P(None, "lat", "lon"),
            P(None, None, "lat", "lon"),
            P(None, "lat", "lon"),
            P("lat", "lon"),
            P("lat", "lon"),
            P(),
            P(),
        ),
        out_specs=(P(None, "lat", "lon"), P(None, None, "lat", "lon"), P(None, "lat", "lon")),
        check_vma=False,
    )
```

```python
import functools
import math

import jax
import jax.numpy as jnp
from jax import lax
from jax.experimental import pallas as pl
from jax.experimental.pallas import tpu as pltpu
from jax.sharding import PartitionSpec as P

GRID_LAT = 3072
GRID_LON = 8640
DEGREES = 1081
STEP_RATIO = 0.05
FRICTION = 0.1

BAND = 48
SLOT = 64
PILE = 8
F32 = jnp.float32
BF16 = jnp.bfloat16
MESH = pl.DeviceIdType.MESH
HBM = pltpu.MemorySpace.HBM
PRE = 8


def iota(shape, dim):
    return lax.broadcasted_iota(jnp.int32, shape, dim)


def halves(x):
    high = x.astype(BF16)
    return high, (x - high.astype(F32)).astype(BF16)


def rows_dot(a, b):
    return lax.dot_general(a, b, (((1,), (0,)), ((), ())), preferred_element_type=F32)


def rows_dot_t(a, b):
    return lax.dot_general(a, b, (((1,), (1,)), ((), ())), preferred_element_type=F32)


def circle(phase, period):
    turns = jnp.floor(phase * (4.0 / period) + 0.5)
    t = (phase - turns * (period / 4.0)) * (2.0 * math.pi / period)
    t2 = t * t
    s = t * (1.0 + t2 * (-1.0 / 6 + t2 * (1.0 / 120 + t2 * (-1.0 / 5040 + t2 * (1.0 / 362880)))))
    c = 1.0 + t2 * (-0.5 + t2 * (1.0 / 24 + t2 * (-1.0 / 720 + t2 * (1.0 / 40320))))
    quarter = turns.astype(jnp.int32) & 3
    odd = (quarter & 1) == 1
    cosine = jnp.where(odd, s, c)
    sine = jnp.where(odd, c, s)
    cosine = jnp.where((quarter == 1) | (quarter == 2), -cosine, cosine)
    sine = jnp.where(quarter >= 2, -sine, sine)
    return cosine, sine


def spectral_kernel(
    bands, sectors, width, wide, length,
    elevation, velocity, wind, depth, mask, love, waves_hbm,
    out_spec, out_th, out_tl, out_fields, out_sine,
    numbers, fields, mask_v, love_v, x_pad, part, piece_in, coef, coef_in,
    back_out, row_msg, row_in, col_msg, col_in,
    ladder_v, ladder_s, raw, table_h, table_l, spec_in,
    load_sem, a_send, a_recv, c_send, c_recv, s_send, s_recv, h_send, h_recv,
):
    depths = bands // PILE
    lows = sectors // 2
    share = 4 * sectors
    band = lax.axis_index("lat")
    sector = lax.axis_index("lon")
    z, x, half = band // 8, (band // 2) % 4, band % 2
    low, core = sector // 2, sector % 2

    sources = [
        (waves_hbm, numbers), (mask, mask_v), (elevation.at[0], fields.at[0]), (love, love_v),
        (velocity.at[0, 0], fields.at[1]), (velocity.at[0, 1], fields.at[2]),
        (wind.at[0], fields.at[3]), (wind.at[1], fields.at[4]), (depth, fields.at[5]),
    ]
    loads = [pltpu.make_async_copy(a, b, load_sem.at[i]) for i, (a, b) in enumerate(sources)]
    for copy in loads[:3]:
        copy.start()

    above = ((band + bands - 1) % bands, sector)
    below = ((band + 1) % bands, sector)
    left = (band, (sector + sectors - 1) % sectors)
    right = (band, (sector + 1) % sectors)

    y = half * lows + low
    place = y * 4 + x

    steps = sorted(
        ((dy, dx, dc) for dy in range(sectors) for dx in range(4) for dc in range(2)
         if dy or dx or dc),
        key=lambda s: -min(s[0], sectors - s[0]) - min(s[1], 4 - s[1]),
    )
    mates = []
    for dy, dx, dc in steps:
        peer_y, peer_x, peer_core = (y + dy) % sectors, (x + dx) % 4, (core + dc) % 2
        peer = (z * 8 + peer_x * 2 + peer_y // lows, (peer_y % lows) * 2 + peer_core)
        mates.append((peer, peer_core, peer_y * 4 + peer_x, peer_x))
    z_steps = sorted(range(1, depths), key=lambda d: -min(d, depths - d))

    plane = [mate[0] for mate in mates]
    z_peers = [(((z + d) % depths) * 8 + x * 2 + half, sector) for d in z_steps]
    peers = plane[:20] + z_peers + plane[20:] + [above, below, left, right]
    barrier = pltpu.get_barrier_semaphore()
    for peer in peers:
        pl.semaphore_signal(barrier, inc=1, device_id=peer, device_id_type=MESH)

    for copy in loads[3:]:
        copy.start()
    x_pad[...] = jnp.zeros_like(x_pad)
    loads[0].wait()

    lane = iota((1, 128), 1)
    sub = iota((16, 128), 0)

    def zonal(s, carry):
        waves = jnp.zeros((16, 128), F32)
        for p in range(16):
            waves = jnp.where(sub == p, numbers[s * 16 + p].astype(F32), waves)
        at = pl.multiple_of((s // (share // 16)) * 2 * share + (s % (share // 16)) * 16, 16)
        for tile in range(wide // 128):
            t = lane + tile * 128
            column = sector * width + jnp.where(t < width + 16, t, t - wide)
            cosine, sine = circle(waves * column.astype(F32), GRID_LON)
            high, low_part = halves(cosine)
            out_th[pl.ds(at, 16), tile * 128 : tile * 128 + 128] = high
            out_tl[pl.ds(at, 16), tile * 128 : tile * 128 + 128] = low_part
            high, low_part = halves(sine)
            out_th[pl.ds(at + share, 16), tile * 128 : tile * 128 + 128] = high
            out_tl[pl.ds(at + share, 16), tile * 128 : tile * 128 + 128] = low_part
        return carry

    lax.fori_loop(0, share // 8, zonal, 0)

    loads[1].wait()
    loads[2].wait()
    x_pad[8:56, 0:width] = fields[0] * mask_v[...].astype(F32)
    x_high, x_low = halves(x_pad[...])
    t_high = out_th[...]
    sums = (
        rows_dot_t(t_high, x_high) + rows_dot_t(t_high, x_low) + rows_dot_t(out_tl[...], x_high)
    )
    slot_row = band * BAND - 8 + iota((1, SLOT), 1)
    slot_sine = circle(slot_row.astype(F32) + 0.5, 2 * GRID_LAT)[1]
    sums = sums * (slot_sine * (math.pi / (2.0 * GRID_LAT) / GRID_LON))
    for c in range(2):
        for kind in range(2):
            at = (2 * c + kind) * share
            part[c, kind] = sums[at : at + share]

    pl.semaphore_wait(barrier, len(peers))
    sends = []

    def send(src, dst, send_sem, recv_sem, peer):
        copy = pltpu.make_async_remote_copy(
            src_ref=src, dst_ref=dst, send_sem=send_sem, recv_sem=recv_sem,
            device_id=peer, device_id_type=MESH,
        )
        copy.start()
        sends.append(copy)
        return copy

    slot = 2 * x + half
    moved = [
        send(part.at[c, :, t], piece_in.at[sector, :, slot], a_send.at[n], a_recv.at[n], peer)
        for n, (peer, c, t, _) in enumerate(mates)
    ]
    piece_in[sector, :, pl.ds(slot, 1), :] = part[core, :, pl.ds(place, 1), :]

    number = numbers[core * share + place]
    order = number.astype(F32)
    degree = (iota((16, 128), 0) * 128 + iota((16, 128), 1)).astype(F32)
    active = degree > order
    gap = jnp.where(active, degree * degree - order * order, 1.0)
    raising = jnp.sqrt((4.0 * degree * degree - 1.0) / gap)
    lower = degree - 1.0
    under = jnp.where(active, lower * lower - order * order, 0.0)
    over = jnp.where(active, 4.0 * lower * lower - 1.0, 1.0)
    raising = jnp.where(active, raising, 0.0)
    ladder_v[0:16, :] = raising
    ladder_v[16:32, :] = raising * jnp.sqrt(under / over)
    to_scalar = pltpu.make_async_copy(ladder_v, ladder_s, load_sem.at[len(sources)])
    to_scalar.start()

    for i in range(3, len(sources)):
        loads[i].wait()
    wet = mask_v[...].astype(F32)
    row_msg[0, 0:2, :] = fields[0, 0:2, :]
    row_msg[1, 0:2, :] = fields[0, BAND - 2 : BAND, :]
    for slot, index in ((2, 1), (3, 2), (4, 4), (5, 5)):
        row_msg[0, slot : slot + 1, :] = fields[index, 0:1, :]
        row_msg[1, slot : slot + 1, :] = fields[index, BAND - 1 : BAND, :]
    row_msg[0, 6:7, :] = wet[0:1]
    row_msg[1, 6:7, :] = wet[BAND - 1 : BAND]
    for slot, index in ((0, 0), (1, 1), (2, 2), (3, 3), (4, 5)):
        col_msg[0, :, 2 * slot : 2 * slot + 2] = fields[index, :, 0:2]
        col_msg[1, :, 2 * slot : 2 * slot + 2] = fields[index, :, width - 2 : width]
    col_msg[0, :, 10:12] = wet[:, 0:2]
    col_msg[1, :, 10:12] = wet[:, width - 2 : width]

    rims = [
        send(row_msg.at[0], row_in.at[1], h_send.at[0], h_recv.at[0], above),
        send(row_msg.at[1], row_in.at[0], h_send.at[1], h_recv.at[1], below),
        send(col_msg.at[0], col_in.at[1], h_send.at[2], h_recv.at[2], left),
        send(col_msg.at[1], col_in.at[0], h_send.at[3], h_recv.at[3], right),
    ]

    row = (z * 8 + 2 * iota((4, 128), 0) + iota((4, 128), 1) // SLOT) * BAND - 8
    row = row + iota((4, 128), 1) % SLOT
    cosine, sine = circle(row.astype(F32) + 0.5, 2 * GRID_LAT)
    ladder = (lane + 1).astype(F32)
    ratio = jnp.where(
        (lane >= 1) & (ladder <= order), jnp.log((2.0 * ladder + 1.0) / (2.0 * ladder)), 0.0
    )
    norm = jnp.sum(ratio, axis=1, keepdims=True) + jnp.where(order > 0.0, math.log(3.0), 0.0)
    log_scale = 0.5 * norm + order * jnp.log(jnp.abs(sine))
    to_scalar.wait()

    def block(inject, i, carry):
        current, previous, scale = carry
        base = pl.multiple_of(i * 16, 16)
        line, first = i // 8, (i % 8) * 16
        root = jnp.exp(0.5 * scale)
        for t in range(16):
            rest = ladder_s[16 + line, first + t] * previous
            if inject:
                rest = rest - jnp.where(base + t == number, 1.0, 0.0)
            latest = (ladder_s[line, first + t] * cosine) * current - rest
            raw[4 * t : 4 * t + 4, :] = latest
            current, previous = latest, current
        for k in range(4):
            factor = root[k : k + 1]
            high, low = halves(raw[pl.ds(k, 16, stride=4), :] * factor * factor)
            table_h[pl.ds(base, 16), 128 * k : 128 * k + 128] = high
            table_l[pl.ds(base, 16), 128 * k : 128 * k + 128] = low
        large = jnp.maximum(jnp.abs(current), jnp.abs(previous)) > 2.0**20
        factor = jnp.where(large, 2.0**-40, 1.0)
        shift = jnp.where(large, 40.0 * math.log(2.0), 0.0)
        return current * factor, previous * factor, scale + shift

    zero = jnp.zeros((4, 128), F32)
    blocks = length // 16
    early = min(8, blocks)
    state = (zero, zero, log_scale)
    state = lax.fori_loop(0, early, functools.partial(block, True), state)
    state = lax.fori_loop(early, min(PRE, blocks), functools.partial(block, False), state)

    lax.fori_loop(min(PRE, blocks), blocks, functools.partial(block, False), state)

    for copy in reversed(moved):
        copy.wait_recv()
    total = piece_in[0]
    for s in range(1, sectors):
        total = total + piece_in[s]
    rows = jnp.concatenate([total[:, k] for k in range(8)], axis=1)
    high = rows.astype(BF16).astype(F32)
    rows = jnp.concatenate([high, rows - high], axis=0).astype(BF16)
    cut = max(128, length // 3 // 128 * 128 + 128)
    parts = [slice(at, min(at + cut, length)) for at in range(0, length, cut)]
    gathered = []
    for h, part_rows in enumerate(parts):
        product = rows_dot_t(rows, table_h[part_rows, :]) + rows_dot_t(rows, table_l[part_rows, :])
        coef[:, part_rows] = product[0:2] + product[2:4]
        gathered.append([
            send(coef.at[:, part_rows], coef_in.at[d, :, part_rows], c_send.at[h, d],
                 c_recv.at[h, d], peer)
            for d, peer in zip(z_steps, z_peers)
        ])

    for copy in rims:
        copy.wait_recv()
    sub_row = band * BAND - 8 + iota((SLOT, 128), 0)
    band_sine = circle(sub_row.astype(F32) + 0.5, 2 * GRID_LAT)[1]
    out_sine[...] = band_sine
    body = slice(8, 8 + BAND)
    for index in range(6):
        out_fields[index, body, 0:width] = fields[index]
    out_fields[6, body, 0:width] = wet
    out_fields[0, 6:8, 0:width] = row_in[0, 0:2, :]
    out_fields[0, 56:58, 0:width] = row_in[1, 0:2, :]
    for slot, index in ((2, 1), (3, 2), (4, 4), (5, 5), (6, 6)):
        out_fields[index, 7:8, 0:width] = row_in[0, slot : slot + 1, :]
        out_fields[index, 56:57, 0:width] = row_in[1, slot : slot + 1, :]
    for slot, index in ((0, 0), (1, 1), (2, 2), (3, 3), (4, 5), (5, 6)):
        out_fields[index, body, wide - 2 : wide] = col_in[0, :, 2 * slot : 2 * slot + 2]
        out_fields[index, body, width : width + 2] = col_in[1, :, 2 * slot : 2 * slot + 2]
    meridional = 0.1 * GRID_LAT / GRID_LON

    def prepare(r, carry):
        at = pl.ds(pl.multiple_of(8 * r, 8), 8)
        u = out_fields[1, at, :]
        v = out_fields[2, at, :]
        inverse = 1.0 / out_fields[5, at, :]
        damping = 1.0 + FRICTION * jnp.sqrt(u * u + v * v) * inverse
        share = out_fields[6, at, :] / damping
        zonal_step = STEP_RATIO / out_sine[at, 0:1]
        out_fields[1, at, :] = share * (u + out_fields[3, at, :] * inverse)
        out_fields[2, at, :] = share * zonal_step
        out_fields[3, at, :] = share * (v + out_fields[4, at, :] * inverse)
        out_fields[4, at, :] = share * meridional
        return carry

    lax.fori_loop(0, SLOT // 8, prepare, 0)
    for copy in reversed(sends):
        copy.wait_send()
    sends.clear()

    degrees = love_v.shape[0]
    weight = love_v[...].reshape(1, degrees) / (2.0 * iota((1, degrees), 1).astype(F32) + 1.0)
    weight = jnp.concatenate([weight, jnp.zeros((1, length - degrees), F32)], axis=1)
    product = 0.0
    for part_rows, copies in zip(parts, gathered):
        for copy in reversed(copies):
            copy.wait_recv()
        whole = coef[:, part_rows]
        for d in range(1, depths):
            whole = whole + coef_in[d, :, part_rows]
        whole = whole * weight[:, part_rows]
        high = whole.astype(BF16).astype(F32)
        whole = jnp.concatenate([high, whole - high], axis=0).astype(BF16)
        product = product + rows_dot(whole, table_h[part_rows, :])
        product = product + rows_dot(whole, table_l[part_rows, :])
    product = product[0:2] + product[2:4]
    for k in range(4):
        back_out[k] = product[:, 128 * k : 128 * k + 128]
    returned = [
        send(back_out.at[k], spec_in.at[core, :, place], s_send.at[n], s_recv.at[n], peer)
        for n, (peer, _, _, k) in enumerate(mates)
    ]
    spec_in[core, :, pl.ds(place, 1), :] = back_out[x].reshape(2, 1, 128)
    for copy in reversed(sends):
        copy.wait_send()
    for copy in reversed(returned):
        copy.wait_recv()
    for c in range(2):
        out_spec[c] = spec_in[c].reshape(2 * share, 128)


def update_kernel(
    bands, width, wide,
    spec, th, tl, fields, sine,
    new_elevation, new_velocity, loading,
    surface, south_flux, loads, results, out_sem,
):
    band = lax.axis_index("lat")
    copies = []

    def store(index, target, rows):
        copy = pltpu.make_async_copy(
            results.at[index, rows], target.at[rows], out_sem.at[len(copies)]
        )
        copy.start()
        copies.append(copy)

    source = iota((SLOT, 128), 0) + SLOT * (band % 2)
    move = jnp.where(iota((SLOT, 128), 1) == source, 1.0, 0.0).astype(BF16)
    high, low = halves(spec[...].reshape(th.shape[0], 128))
    high = rows_dot_t(move, high).astype(BF16)
    low = rows_dot_t(move, low).astype(BF16)
    t_high = th[...]
    loads[...] = rows_dot(high, t_high) + rows_dot(low, t_high) + rows_dot(high, tl[...])

    meridional = 0.1 * GRID_LAT / GRID_LON
    sub = iota((8, 1), 0)
    for r in range(8):
        at = slice(8 * r, 8 * r + 8)
        row = band * BAND - 8 + 8 * r + sub
        inside = (row >= 0) & (row < GRID_LAT)
        load = loads[at, :]
        surface[8 + 8 * r : 16 + 8 * r, :] = jnp.where(inside, fields[0, at, :] - load, 0.0)
        if 1 <= r <= 6:
            results[0, 8 * r - 8 : 8 * r, :] = load[:, 0:width]
    store(0, loading.at[0], pl.ds(0, BAND))
    for r in range(8):
        at = slice(8 * r, 8 * r + 8)
        row = band * BAND - 8 + 8 * r + sub
        inside = (row >= 0) & (row < GRID_LAT)
        change = surface[9 + 8 * r : 17 + 8 * r, :] - surface[7 + 8 * r : 15 + 8 * r, :]
        new_v = fields[3, at, :] - fields[4, at, :] * change
        flux = sine[at, 0:1] * fields[5, at, :] * new_v
        south_flux[at, :] = jnp.where(inside, flux, 0.0)
        if 1 <= r <= 6:
            results[1, 8 * r - 8 : 8 * r, :] = new_v[:, 0:width]
    store(1, new_velocity.at[0, 1], pl.ds(0, BAND))
    for r in range(1, 7):
        at = slice(8 * r, 8 * r + 8)
        here = surface[8 + 8 * r : 16 + 8 * r, :]
        change = pltpu.roll(here, wide - 1, 1) - pltpu.roll(here, 1, 1)
        new_u = fields[1, at, :] - fields[2, at, :] * change
        flux = fields[5, at, :] * new_u
        east = pltpu.roll(flux, wide - 1, 1) - pltpu.roll(flux, 1, 1)
        down = south_flux[8 * r + 1 : 8 * r + 9, :] - south_flux[8 * r - 1 : 8 * r + 7, :]
        row_sine = sine[at, 0:1]
        tendency = (STEP_RATIO / row_sine) * east + (meridional / row_sine) * down
        level = fields[0, at, :] - fields[6, at, :] * tendency
        results[2, 8 * r - 8 : 8 * r, :] = new_u[:, 0:width]
        results[3, 8 * r - 8 : 8 * r, :] = level[:, 0:width]
        if r % 2 == 0:
            store(2, new_velocity.at[0, 0], pl.ds(8 * r - 16, 16))
            store(3, new_elevation.at[0], pl.ds(8 * r - 16, 16))
    for copy in copies:
        copy.wait()


def local(bands, sectors, elevation, velocity, wind_forcing, ocean_depth, wet_mask, love_factor,
          wavenumbers):
    width = elevation.shape[2]
    wide = -(-(width + 18) // 128) * 128
    length = -(-DEGREES // 16) * 16
    depths = bands // PILE
    share = 4 * sectors
    vmem = pl.BlockSpec(memory_space=pltpu.VMEM)
    hbm = pl.BlockSpec(memory_space=HBM)
    dma = pltpu.SemaphoreType.DMA
    shared = pl.pallas_call(
        functools.partial(spectral_kernel, bands, sectors, width, wide, length),
        out_shape=[
            jax.ShapeDtypeStruct((2, 2 * share, 128), F32),
            jax.ShapeDtypeStruct((4 * share, wide), BF16),
            jax.ShapeDtypeStruct((4 * share, wide), BF16),
            jax.ShapeDtypeStruct((7, SLOT, wide), F32),
            jax.ShapeDtypeStruct((SLOT, 128), F32),
        ],
        in_specs=[hbm] * 7,
        out_specs=[vmem] * 5,
        scratch_shapes=[
            pltpu.SMEM((8 * sectors,), jnp.int32),
            pltpu.VMEM((6, BAND, width), F32),
            pltpu.VMEM((BAND, width), jnp.int32),
            pltpu.VMEM((DEGREES,), F32),
            pltpu.VMEM((SLOT, wide), F32),
            pltpu.VMEM((2, 2, share, SLOT), F32),
            pltpu.VMEM((sectors, 2, 8, SLOT), F32),
            pltpu.VMEM((2, length), F32),
            pltpu.VMEM((depths, 2, length), F32),
            pltpu.VMEM((4, 2, 128), F32),
            pltpu.VMEM((2, 8, width), F32),
            pltpu.VMEM((2, 8, width), F32),
            pltpu.VMEM((2, BAND, 128), F32),
            pltpu.VMEM((2, BAND, 128), F32),
            pltpu.VMEM((32, 128), F32),
            pltpu.SMEM((32, 128), F32),
            pltpu.VMEM((64, 128), F32),
            pltpu.VMEM((length, 512), BF16),
            pltpu.VMEM((length, 512), BF16),
            pltpu.VMEM((2, 2, share, 128), F32),
            dma((10,)),
            dma((2 * share,)), dma((2 * share,)),
            dma((3, depths)), dma((3, depths)),
            dma((2 * share,)), dma((2 * share,)),
            dma((4,)), dma((4,)),
        ],
        compiler_params=pltpu.CompilerParams(
            collective_id=0, has_side_effects=True, vmem_limit_bytes=24 * 1024 * 1024
        ),
        name="spectral",
    )(*[
        pltpu.with_memory_space_constraint(array, HBM)
        for array in (elevation, velocity, wind_forcing, ocean_depth, wet_mask,
                      love_factor, wavenumbers)
    ])
    return pl.pallas_call(
        functools.partial(update_kernel, bands, width, wide),
        out_shape=[
            jax.ShapeDtypeStruct(elevation.shape, F32),
            jax.ShapeDtypeStruct(velocity.shape, F32),
            jax.ShapeDtypeStruct(elevation.shape, F32),
        ],
        in_specs=[vmem] * 5,
        out_specs=[hbm] * 3,
        scratch_shapes=[
            pltpu.VMEM((SLOT + 16, wide), F32),
            pltpu.VMEM((SLOT, wide), F32),
            pltpu.VMEM((SLOT, wide), F32),
            pltpu.VMEM((4, BAND, width), F32),
            dma((8,)),
        ],
        compiler_params=pltpu.CompilerParams(vmem_limit_bytes=24 * 1024 * 1024),
        name="update",
    )(*shared)


def solution(mesh):
    bands, sectors = mesh.shape["lat"], mesh.shape["lon"]
    return jax.shard_map(
        functools.partial(local, bands, sectors),
        mesh=mesh,
        in_specs=(
            P(None, "lat", "lon"),
            P(None, None, "lat", "lon"),
            P(None, "lat", "lon"),
            P("lat", "lon"),
            P("lat", "lon"),
            P(),
            P(),
        ),
        out_specs=(P(None, "lat", "lon"), P(None, None, "lat", "lon"), P(None, "lat", "lon")),
        check_vma=False,
    )
```
